128 devices in a mesh: section: 8 (over y_hi, x), dp: 16 (over z, y_lo, core).
Axes of the slice: x: 4, y: 4 (y_hi: 2, y_lo: 2; y = y_hi * 2 + y_lo), z: 4, core: 2. Of those that a mesh axis runs over, the one named last changes fastest.
Arguments:
- tokens: bfloat16 [2, 2048, 2048], P(None, 'dp'), may hold values from -12 to 12
- cotangent: bfloat16 [2, 2048, 2048], P(None, 'dp'), may hold values from -12 to 12
- gain: float32 [8, 2048], P('section'), may hold values from 0.3 to 3
- weight: bfloat16 [16384, 2048], P('section'), may hold values from -0.125 to 0.125
Outputs:
- act_roots: float32 [8192, 2048], P(('section', 'dp'))
- grad_roots: float32 [8192, 2048], P(('section', 'dp'))
The draws below stay inside these ranges and needn't reach their ends.
All inputs are finite; a program needn't handle non-finite values. Where the reference program divides by a largest or mean magnitude, that divisor is 1e-20 or more.
Results may differ from the reference program's by a relative error of at most 0.00085.
Values may be sent and summed in bfloat16 or wider, within the bound.
A program may use at most 128 MiB of HBM per device.

```python
import math
import jax
import jax.numpy as jnp
from jax import lax

D = 2048
BLK = 1024
MB = 2
TOKENS = 2048
SECTIONS = 8


def draw_tokens(key, part):
    key = jax.random.fold_in(key, 11)
    scale_key, value_key = jax.random.split(key)
    spread = jnp.exp(jax.random.uniform(scale_key, (D,), jnp.float32, math.log(0.3), math.log(3.0)))
    values = jnp.clip(jax.random.normal(value_key, (MB, TOKENS, D), jnp.float32), -4.0, 4.0)
    return (values * spread).astype(jnp.bfloat16)


def draw_cotangent(key, part):
    key = jax.random.fold_in(key, 12)
    scale_key, value_key = jax.random.split(key)
    spread = jnp.exp(jax.random.uniform(scale_key, (D,), jnp.float32, math.log(0.3), math.log(3.0)))
    values = jnp.clip(jax.random.normal(value_key, (MB, TOKENS, D), jnp.float32), -4.0, 4.0)
    return (values * spread).astype(jnp.bfloat16)


def shard_levels(stream_key, dims, shards, least, top_value):
    def one(dim, parts):
        steps = jax.random.uniform(jax.random.fold_in(jax.random.fold_in(stream_key, 6), dim), (parts,), jnp.float32, least / len(shards), top_value / len(shards))
        return jnp.repeat(jnp.exp(steps), dims[dim] // parts).reshape((-1,) + (1,) * (len(dims) - dim - 1))

    level = one(*shards[0])
    for cut in shards[1:]:
        level = level * one(*cut)
    return level


def centred(rng, shape, scale, limit, cuts=(), kind=jnp.bfloat16):
    array = jax.random.normal(rng, shape, jnp.float32) * scale
    if len(cuts) > 0:
        array = shard_levels(rng, shape, cuts, -0.22, 0.18) * array
    return jnp.clip(array, min=-limit, max=limit).astype(kind)


def setup_inputs(seed: int = 0) -> dict:
    arg_keys = jax.random.split(jax.random.key(seed), 5)
    tokens = draw_tokens(jax.random.fold_in(arg_keys[4], 71), 0)
    cotangent = draw_cotangent(jax.random.fold_in(arg_keys[4], 71), 0)
    gain = jnp.clip(jnp.exp(math.log(3.0) - 2.3025851 * jax.random.uniform(arg_keys[2], (SECTIONS, D), jnp.float32) ** shard_levels(arg_keys[2], (SECTIONS, D), ((0, 8),), -0.2, 0.2)), 0.3, 3.0)
    weight = centred(arg_keys[3], (SECTIONS * D, D), D ** -0.5, 0.125, ((0, 8),))
    return dict(tokens=tokens, cotangent=cotangent, gain=gain, weight=weight)


damping_term = 4.0

def gelu_tanh(values):
    return jax.nn.gelu(values, approximate=True)

def layer_forward(inputs, scale_row, matrix):
    widened = inputs.astype(jnp.float32)
    inverse_rms = lax.rsqrt(lax.optimization_barrier(jnp.mean(widened * widened, axis=-1, keepdims=True)) + 1e-06)
    normed = (widened * inverse_rms * scale_row).astype(jnp.bfloat16)
    preact = jnp.dot(normed, matrix, preferred_element_type=jnp.float32)
    outputs = (widened + gelu_tanh(preact)).astype(jnp.bfloat16)
    return (normed, preact, outputs)

def layer_backward(inputs, preact, upstream, scale_row, matrix):
    widened = inputs.astype(jnp.float32)
    inverse_rms = lax.rsqrt(lax.optimization_barrier(jnp.mean(widened * widened, axis=-1, keepdims=True)) + 1e-06)
    upward = upstream.astype(jnp.float32)
    pullback = jax.vjp(gelu_tanh, preact)[1]
    deltas = pullback(upward)[0].astype(jnp.bfloat16)
    backprop = lax.dot_general(deltas, matrix, (((1,), (1,)), ((), ())), preferred_element_type=jnp.float32)
    normal_hat = widened * inverse_rms
    scaled = backprop * scale_row
    downward = upward + inverse_rms * (scaled - normal_hat * lax.optimization_barrier(jnp.mean(scaled * normal_hat, axis=-1, keepdims=True)))
    return (deltas, downward.astype(jnp.bfloat16))

def inverse_root(factor):
    highest = lax.Precision.HIGHEST
    identity = jnp.eye(BLK, dtype=jnp.float32)
    row_bound = jnp.max(lax.optimization_barrier(jnp.sum(jnp.abs(factor), axis=1)))
    scaled_start = factor / row_bound
    first_step = 1.5 * identity - 0.5 * scaled_start
    middle = jnp.dot(scaled_start, first_step, precision=highest)
    square = jnp.dot(middle, first_step, precision=highest)
    second = 1.5 * identity - 0.5 * square
    return jnp.dot(second, first_step, precision=highest)

def factor_roots(matrix_rows):
    results = []
    for block_index in range(D // BLK):
        columns = matrix_rows[:, block_index * BLK:(block_index + 1) * BLK]
        gram_block = jnp.dot(columns.T, columns, preferred_element_type=jnp.float32)
        damped = gram_block / (MB * TOKENS) + damping_term * jnp.eye(BLK, dtype=jnp.float32)
        results.append(inverse_root(damped))
    return jnp.concatenate(results, axis=1)

def reference(tokens, cotangent, gain, weight):
    row_total = MB * TOKENS
    current = tokens.reshape(row_total, D)
    saved = []
    act_rows = []
    for section in range(SECTIONS):
        matrix = weight[section * D:(section + 1) * D]
        normed, preact, outputs = layer_forward(current, gain[section], matrix)
        saved.append((current, preact))
        act_rows.append(factor_roots(normed))
        current = outputs
    upstream = cotangent.reshape(row_total, D)
    grad_rows = [None] * SECTIONS
    for section in reversed(range(SECTIONS)):
        current, preact = saved[section]
        matrix = weight[section * D:(section + 1) * D]
        deltas, upstream = layer_backward(current, preact, upstream, gain[section], matrix)
        grad_rows[section] = factor_roots(deltas)
    return (jnp.concatenate(act_rows, axis=0), jnp.concatenate(grad_rows, axis=0))
```

```python
import functools

import jax
import jax.numpy as jnp
from jax import lax
from jax.experimental import pallas as pl
from jax.experimental.pallas import tpu as pltpu
from jax.sharding import PartitionSpec as P

MESH = pl.DeviceIdType.MESH
F32 = jnp.float32
BF16 = jnp.bfloat16

D = 2048
BLK = 1024
ROWS = 256
R = 32
M = ROWS // R
TN = 256
NT = D // TN
CHIPS = 8
SLAB = BLK // CHIPS
HALF = SLAB // 2
KEPT = 5
ROW_TOTAL = 4096.0
DAMPING = 4.0
SECTIONS = 8
LAG = 3

GELU_A = 0.7978845608028654
GELU_B = 0.044715


def gelu_value(z):
    t = jnp.tanh(GELU_A * (z + GELU_B * (z * z * z)))
    return 0.5 * z * (1.0 + t)


def gelu_slope(z):
    sq = z * z
    t = jnp.tanh(GELU_A * (z + GELU_B * (sq * z)))
    return 0.5 * (1.0 + t) + 0.5 * z * (1.0 - t * t) * (GELU_A * (1.0 + 3.0 * GELU_B * sq))


def kernel(
    tok, cot, gain, wgt, act_out, grad_out,
    w, wt, xs, ys, sendf, sendb, zs, ns, ds, rinvs, sib, gram, rs, ag, full, slab, ztile,
    w_sem, tok_sem, f_send, f_recv, b_send, b_recv, sib_send, sib_recv,
    rs_send, rs_recv, ag_send, ag_recv, own_sem, out_send, out_recv,
):
    s = lax.axis_index("section")
    d = lax.axis_index("dp")
    chip = d // 2
    core = d % 2
    nxt = (jnp.minimum(s + 1, SECTIONS - 1), d)
    prv = (jnp.maximum(s - 1, 0), d)
    sibling = (s, chip * 2 + 1 - core)
    first = s == 0
    last = s == SECTIONS - 1

    def peer(k):
        return (s, k * 2 + core)

    def w_copy(j):
        cols = pl.ds(j * TN, TN)
        return pltpu.make_async_copy(wgt.at[:, cols], w.at[:, cols], w_sem.at[j])

    for j in range(NT):
        w_copy(j).start()

    def rows_copy(source, target, j):
        half = ROWS // 2
        return [
            pltpu.make_async_copy(
                source.at[mb, :, pl.ds(j * TN, TN)], target.at[j, pl.ds(mb * half, half), :], tok_sem.at[j * 2 + mb]
            )
            for mb in range(2)
        ]

    @pl.when(first)
    def _():
        for j in range(NT):
            for cp in rows_copy(tok, xs, j):
                cp.start()

    @pl.when(last)
    def _():
        for j in range(NT):
            for cp in rows_copy(cot, ys, j):
                cp.start()

    barrier = pltpu.get_barrier_semaphore()
    for k in range(1, CHIPS):
        pl.semaphore_signal(barrier, inc=1, device_id=peer((chip + k) % CHIPS), device_id_type=MESH)
    pl.semaphore_signal(barrier, inc=1, device_id=sibling, device_id_type=MESH)

    @pl.when(s < SECTIONS - 1)
    def _():
        pl.semaphore_signal(barrier, inc=1, device_id=nxt, device_id_type=MESH)

    @pl.when(s > 0)
    def _():
        pl.semaphore_signal(barrier, inc=1, device_id=prv, device_id_type=MESH)

    pl.semaphore_wait(barrier, CHIPS + jnp.where(first, 0, 1) + jnp.where(last, 0, 1))

    @pl.when(first)
    def _():
        for j in range(NT):
            for cp in rows_copy(tok, xs, j):
                cp.wait()

    @pl.when(last)
    def _():
        for j in range(NT):
            for cp in rows_copy(cot, ys, j):
                cp.wait()

    for j in range(NT):
        w_copy(j).wait()

    def transpose_weight():
        def body(k, _):
            kr = pl.ds(pl.multiple_of(k * TN, TN), TN)
            for j in range(NT):
                wt[j * TN : (j + 1) * TN, kr] = w[kr, j * TN : (j + 1) * TN].T
            return 0

        lax.fori_loop(0, NT, body, 0)

    def chunk_rows(m):
        return pl.ds(pl.multiple_of(m * R, R), R)

    def f_copy(m, part):
        rows = chunk_rows(m)
        return pltpu.make_async_remote_copy(
            src_ref=sendf.at[part, rows, :], dst_ref=xs.at[part, rows, :],
            send_sem=f_send.at[m], recv_sem=f_recv.at[m], device_id=nxt, device_id_type=MESH,
        )

    def b_copy(m, part):
        rows = chunk_rows(m)
        return pltpu.make_async_remote_copy(
            src_ref=sendb.at[part, rows, :], dst_ref=ys.at[part, rows, :],
            send_sem=b_send.at[m], recv_sem=b_recv.at[m], device_id=prv, device_id_type=MESH,
        )

    whole = pl.ds(0, NT)

    def sib_copy(f, m):
        rows = chunk_rows(m)
        store = ns if f == 0 else ds
        return pltpu.make_async_remote_copy(
            src_ref=store.at[rows, pl.ds(pl.multiple_of((1 - core) * BLK, BLK), BLK)], dst_ref=sib.at[f, rows, :],
            send_sem=sib_send.at[f, m], recv_sem=sib_recv.at[f, m], device_id=sibling, device_id_type=MESH,
        )

    def forward(m, send):
        rows = chunk_rows(m)
        total = jnp.zeros((R, TN), F32)
        for j in range(NT):
            xj = xs[j, rows, :].astype(F32)
            total = total + xj * xj
        rinv = lax.rsqrt(jnp.sum(total, axis=-1, keepdims=True) * (1.0 / D) + 1e-06)
        rinvs[rows, :] = jnp.broadcast_to(rinv, (R, 128))
        for j in range(NT):
            cols = slice(j * TN, (j + 1) * TN)
            ns[rows, cols] = (xs[j, rows, :].astype(F32) * rinv * gain[:, cols]).astype(BF16)
        normed = ns[rows, :]
        for j in range(NT):
            cols = slice(j * TN, (j + 1) * TN)
            z = jnp.dot(normed, w[:, cols], preferred_element_type=F32)
            zs[rows, cols] = z
            if send:
                sendf[j, rows, :] = (xs[j, rows, :].astype(F32) + gelu_value(z)).astype(BF16)
                f_copy(m, j).start()
        sib_copy(0, m).start()

    def backward(m, send):
        rows = chunk_rows(m)
        total = jnp.zeros((R, TN), F32)
        for j in range(NT):
            cols = slice(j * TN, (j + 1) * TN)
            z = zs[rows, cols]
            delta = (ys[j, rows, :].astype(F32) * gelu_slope(z)).astype(BF16)
            ds[rows, cols] = delta
            total = total + delta.astype(F32) * z
        if send:
            rinv = rinvs[rows, :1]
            pull = jnp.sum(total, axis=-1, keepdims=True) * (1.0 / D) * rinv
            deltas = ds[rows, :]
            for j in range(NT):
                cols = slice(j * TN, (j + 1) * TN)
                dn = jnp.dot(deltas, wt[:, cols], preferred_element_type=F32)
                xj = xs[j, rows, :].astype(F32)
                dy = ys[j, rows, :].astype(F32) + rinv * (dn * gain[:, cols] - xj * pull)
                sendb[j, rows, :] = dy.astype(BF16)
                b_copy(m, j).start()
        sib_copy(1, m).start()

    def forward_step(m):
        @pl.when(s > 0)
        def _():
            f_copy(m, whole).wait_recv()

        @pl.when(s < SECTIONS - 1)
        def _():
            forward(m, True)

        @pl.when(last)
        def _():
            forward(m, False)

    def backward_step(m):
        @pl.when(s < SECTIONS - 1)
        def _():
            b_copy(m, whole).wait_recv()

        @pl.when(s > 0)
        def _():
            backward(m, True)

        @pl.when(first)
        def _():
            backward(m, False)

    def rs_copy(f, k):
        return pltpu.make_async_remote_copy(
            src_ref=gram.at[f, pl.ds(k, KEPT), pl.ds(pl.multiple_of(k * SLAB, SLAB), SLAB), :],
            dst_ref=rs.at[f, chip],
            send_sem=rs_send.at[f, k], recv_sem=rs_recv.at[f, chip], device_id=peer(k), device_id_type=MESH,
        )

    def rs_arrival(f, k):
        return pltpu.make_async_remote_copy(
            src_ref=rs.at[f, k], dst_ref=rs.at[f, k],
            send_sem=rs_send.at[f, k], recv_sem=rs_recv.at[f, k], device_id=peer(k), device_id_type=MESH,
        )

    def ag_copy(f, k):
        return pltpu.make_async_remote_copy(
            src_ref=ag.at[f, chip], dst_ref=ag.at[f, chip],
            send_sem=ag_send.at[f, k], recv_sem=ag_recv.at[f, chip], device_id=peer(k), device_id_type=MESH,
        )

    def ag_arrival(f, k):
        return pltpu.make_async_remote_copy(
            src_ref=ag.at[f, k], dst_ref=ag.at[f, k],
            send_sem=ag_send.at[f, k], recv_sem=ag_recv.at[f, k], device_id=peer(k), device_id_type=MESH,
        )

    def each_peer(fn):
        def body(k, _):
            fn((chip + k) % CHIPS)
            return 0

        lax.fori_loop(1, CHIPS, body, 0)

    def gram_send(f):
        def landed(m, _):
            sib_copy(f, m).wait_recv()
            return 0

        lax.fori_loop(0, M, landed, 0)
        store = ns if f == 0 else ds
        mine = pl.ds(pl.multiple_of(core * BLK, BLK), BLK)
        own = store[:, mine]
        other = sib[f]
        dims = (((0,), (0,)), ((), ()))
        for q in range(BLK // 256):
            cut = slice(q * 256, (q + 1) * 256)
            own_cut = store[:, pl.ds(pl.multiple_of(core * BLK + q * 256, 256), 256)]
            part = lax.dot_general(own_cut, own, dims, preferred_element_type=F32)
            part = part + lax.dot_general(sib[f, :, cut], other, dims, preferred_element_type=F32)
            part = part.astype(BF16)
            for t in range(CHIPS):
                tile = part[:, t * SLAB : (t + 1) * SLAB]
                gram[f, t, cut, :] = tile
                if t < KEPT - 1:
                    gram[f, t + CHIPS, cut, :] = tile
        each_peer(lambda k: rs_copy(f, k).start())

    def sum_gather(f):
        mine = pl.ds(pl.multiple_of(chip * SLAB, SLAB), SLAB)
        rs[f, chip] = gram[f, pl.ds(chip, KEPT), mine, :]
        each_peer(lambda k: rs_arrival(f, k).wait_recv())
        ri = lax.broadcasted_iota(jnp.int32, (SLAB, SLAB), 0)
        ci = lax.broadcasted_iota(jnp.int32, (SLAB, SLAB), 1)
        eye = ri == ci
        for j in range(KEPT):
            total = rs[f, 0, j].astype(F32)
            for k in range(1, CHIPS):
                total = total + rs[f, k, j].astype(F32)
            total = total * (1.0 / ROW_TOTAL)
            if j == 0:
                diag = jnp.sum(jnp.where(eye, total, 0.0), axis=0, keepdims=True) + DAMPING
                high = diag.astype(BF16).astype(F32)
                row = lax.broadcasted_iota(jnp.int32, (16, SLAB), 0)
                extra = jnp.where(row == 0, high, jnp.where(row == 1, diag - high, 0.0))
                ag[f, chip, KEPT * SLAB : KEPT * SLAB + 16, :] = extra.astype(BF16)
                total = jnp.where(eye, 0.0, total)
            ag[f, chip, j * SLAB : (j + 1) * SLAB, :] = total.astype(BF16)
        each_peer(lambda k: ag_copy(f, k).start())

    def roots(f, out):
        each_peer(lambda k: ag_arrival(f, k).wait_recv())
        pieces = []
        for k in range(CHIPS):
            here = slice(k * SLAB, (k + 1) * SLAB)
            for j in range(KEPT):
                there = (k + j) % CHIPS
                there = slice(there * SLAB, (there + 1) * SLAB)
                tile = ag[f, k, j * SLAB : (j + 1) * SLAB, :]
                full[here, there] = tile
                if 0 < j < KEPT - 1:
                    full[there, here] = tile.T
            extra = ag[f, k, KEPT * SLAB : KEPT * SLAB + 16, :].astype(F32)
            pieces.append(jnp.sum(extra, axis=0, keepdims=True))
        diag = jnp.concatenate(pieces, axis=1)
        bound = jnp.abs(diag)
        for k in range(CHIPS):
            part = jnp.abs(full[k * SLAB : (k + 1) * SLAB, :].astype(F32))
            bound = bound + jnp.sum(part, axis=0, keepdims=True)
        scale = 1.0 / jnp.max(bound, axis=1, keepdims=True)
        mine = pl.ds(pl.multiple_of(chip * SLAB, SLAB), SLAB)
        ri = lax.broadcasted_iota(jnp.int32, (SLAB, BLK), 0)
        ci = lax.broadcasted_iota(jnp.int32, (SLAB, BLK), 1)
        eye = ci == ri + chip * SLAB
        scaled_diag = diag * scale
        off = full[mine, :].astype(F32) * scale
        slab[0] = off
        slab[1] = jnp.where(eye, scaled_diag, off)

        def times(u):
            u_diag = jnp.sum(jnp.where(eye, u, 0.0), axis=1, keepdims=True)
            u_off = jnp.where(eye, 0.0, u).astype(BF16)
            prod = jnp.dot(u_off, full[...], preferred_element_type=F32) * scale
            return prod + u_diag * slab[0] + u * scaled_diag

        u = times(0.0625 * slab[1]) - 0.5625 * slab[1]
        u = times(u) + 1.6875 * slab[1]
        u = times(u) - 2.4375 * slab[1]
        ztile[f] = u + jnp.where(eye, 2.25, 0.0)
        cols = pl.ds(pl.multiple_of(core * BLK, BLK), BLK)
        to_sibling(f, out).start()
        to_out(f, out).start()

    def to_sibling(f, out):
        cols = pl.ds(pl.multiple_of(core * BLK, BLK), BLK)
        return pltpu.make_async_remote_copy(
            src_ref=ztile.at[f, pl.ds(pl.multiple_of((1 - core) * HALF, HALF), HALF), :], dst_ref=out.at[:, cols],
            send_sem=out_send.at[f], recv_sem=out_recv.at[f], device_id=sibling, device_id_type=MESH,
        )

    def to_out(f, out):
        cols = pl.ds(pl.multiple_of(core * BLK, BLK), BLK)
        return pltpu.make_async_copy(
            ztile.at[f, pl.ds(pl.multiple_of(core * HALF, HALF), HALF), :], out.at[:, cols], own_sem.at[f]
        )

    @pl.when(s >= 4)
    def _():
        transpose_weight()

    lag = jnp.minimum(M, (SECTIONS - 1 - s) * LAG)

    def first_half(i, _):
        forward_step(i)

        @pl.when(i >= lag)
        def _():
            backward_step(i - lag)

        return 0

    lax.fori_loop(0, M, first_half, 0)

    @pl.when((s >= 1) & (s < 4))
    def _():
        transpose_weight()

    @pl.when(s <= 4)
    def _():
        gram_send(0)

    @pl.when(s <= 1)
    def _():
        sum_gather(0)
        roots(0, act_out)

    def second_half(i, _):
        backward_step(i)
        return 0

    lax.fori_loop(M - lag, M, second_half, 0)

    @pl.when(s >= 5)
    def _():
        gram_send(0)

    gram_send(1)

    @pl.when(s >= 2)
    def _():
        sum_gather(0)

    sum_gather(1)

    @pl.when(s >= 2)
    def _():
        roots(0, act_out)

    roots(1, grad_out)

    for f, out in ((0, act_out), (1, grad_out)):
        to_out(f, out).wait()
        to_sibling(f, out).wait()

    def sent(m, _):
        @pl.when(s < SECTIONS - 1)
        def _():
            f_copy(m, whole).wait_send()

        @pl.when(s > 0)
        def _():
            b_copy(m, whole).wait_send()

        sib_copy(0, m).wait_send()
        sib_copy(1, m).wait_send()
        return 0

    lax.fori_loop(0, M, sent, 0)
    for f in range(2):
        each_peer(lambda k: rs_copy(f, k).wait_send())
        each_peer(lambda k: ag_copy(f, k).wait_send())


def shards(tokens, cotangent, gain, weight):
    out = jax.ShapeDtypeStruct((HALF, D), F32)
    dma = pltpu.SemaphoreType.DMA
    anywhere = pl.BlockSpec(memory_space=pl.ANY)
    return pl.pallas_call(
        kernel,
        out_shape=(out, out),
        in_specs=[anywhere, anywhere, pl.BlockSpec(memory_space=pltpu.VMEM), anywhere],
        out_specs=(anywhere, anywhere),
        scratch_shapes=[
            pltpu.VMEM((D, D), BF16),
            pltpu.VMEM((D, D), BF16),
            pltpu.VMEM((NT, ROWS, TN), BF16),
            pltpu.VMEM((NT, ROWS, TN), BF16),
            pltpu.VMEM((NT, ROWS, TN), BF16),
            pltpu.VMEM((NT, ROWS, TN), BF16),
            pltpu.VMEM((ROWS, D), F32),
            pltpu.VMEM((ROWS, D), BF16),
            pltpu.VMEM((ROWS, D), BF16),
            pltpu.VMEM((ROWS, 128), F32),
            pltpu.VMEM((2, ROWS, BLK), BF16),
            pltpu.VMEM((2, CHIPS + KEPT - 1, BLK, SLAB), BF16),
            pltpu.VMEM((2, CHIPS, KEPT, SLAB, SLAB), BF16),
            pltpu.VMEM((2, CHIPS, KEPT * SLAB + 16, SLAB), BF16),
            pltpu.VMEM((BLK, BLK), BF16),
            pltpu.VMEM((2, SLAB, BLK), F32),
            pltpu.VMEM((2, SLAB, BLK), F32),
            dma((NT,)),
            dma((2 * NT,)),
            dma((M,)),
            dma((M,)),
            dma((M,)),
            dma((M,)),
            dma((2, M)),
            dma((2, M)),
            dma((2, CHIPS)),
            dma((2, CHIPS)),
            dma((2, CHIPS)),
            dma((2, CHIPS)),
            dma((2,)),
            dma((2,)),
            dma((2,)),
        ],
        name="refresh",
        compiler_params=pltpu.CompilerParams(
            collective_id=0, has_side_effects=True, vmem_limit_bytes=58 * 2**20
        ),
    )(tokens, cotangent, gain, weight)


def solution(mesh):
    return jax.shard_map(
        shards,
        mesh=mesh,
        in_specs=(P(None, "dp", None), P(None, "dp", None), P("section", None), P("section", None)),
        out_specs=(P(("section", "dp"), None), P(("section", "dp"), None)),
        check_vma=False,
    )
```

```python
import functools

import jax
import jax.numpy as jnp
from jax import lax
from jax.experimental import pallas as pl
from jax.experimental.pallas import tpu as pltpu
from jax.sharding import PartitionSpec as P

MESH = pl.DeviceIdType.MESH
F32 = jnp.float32
BF16 = jnp.bfloat16

D = 2048
BLK = 1024
ROWS = 256
R = 32
M = ROWS // R
TN = 256
NT = D // TN
CHIPS = 8
SLAB = BLK // CHIPS
HALF = SLAB // 2
KEPT = 5
ROW_TOTAL = 4096.0
DAMPING = 4.0
SECTIONS = 8
LAG = 3
PAD = 128
EACH = 4

GELU_A = 0.7978845608028654
GELU_B = 0.044715


def gelu_value(z):
    t = jnp.tanh(GELU_A * (z + GELU_B * (z * z * z)))
    return 0.5 * z * (1.0 + t)


def gelu_slope(z):
    sq = z * z
    t = jnp.tanh(GELU_A * (z + GELU_B * (sq * z)))
    return 0.5 * (1.0 + t) + 0.5 * z * (1.0 - t * t) * (GELU_A * (1.0 + 3.0 * GELU_B * sq))


def kernel(
    tok, cot, gain, wgt, act_out, grad_out,
    w, wt, xs, ys, sendf, sendb, zs, ns, ds, rinvs, sib, gram, rs, ag, full, slab, ztile, lhs,
    w_sem, tok_sem, f_send, f_recv, b_send, b_recv, sib_send, sib_recv,
    rs_send, rs_recv, ag_send, ag_recv, own_sem, out_send, out_recv,
):
    s = lax.axis_index("section")
    d = lax.axis_index("dp")
    chip = d // 2
    core = d % 2
    nxt = (jnp.minimum(s + 1, SECTIONS - 1), d)
    prv = (jnp.maximum(s - 1, 0), d)
    sibling = (s, chip * 2 + 1 - core)
    first = s == 0
    last = s == SECTIONS - 1

    def peer(k):
        return (s, k * 2 + core)

    def w_copy(j):
        cols = pl.ds(j * TN, TN)
        return pltpu.make_async_copy(wgt.at[:, cols], w.at[:, cols], w_sem.at[j])

    def first_load(source, target, j):
        cols = pl.ds(j * TN, TN)
        return pltpu.make_async_copy(source.at[0, :, cols], target.at[0, j], tok_sem.at[0])

    def rest_load(source, target, j):
        cols = pl.ds(j * TN, TN)
        return pltpu.make_async_copy(source.at[1:M, :, cols], target.at[1:M, j], tok_sem.at[1])

    def loaded(target, m):
        @pl.when(m == 0)
        def _():
            pltpu.make_async_copy(target.at[0], target.at[0], tok_sem.at[0]).wait()

        @pl.when(m == 1)
        def _():
            pltpu.make_async_copy(target.at[1:M], target.at[1:M], tok_sem.at[1]).wait()

    @pl.when(first)
    def _():
        for j in range(NT):
            first_load(tok, xs, j).start()

    for j in range(NT):
        w_copy(j).start()

    @pl.when(first)
    def _():
        for j in range(NT):
            rest_load(tok, xs, j).start()

    @pl.when(last)
    def _():
        for j in range(NT):
            first_load(cot, ys, j).start()
            rest_load(cot, ys, j).start()

    lhs[...] = jnp.zeros_like(lhs)

    barrier = pltpu.get_barrier_semaphore()
    for k in range(1, CHIPS):
        pl.semaphore_signal(barrier, inc=1, device_id=peer((chip + k) % CHIPS), device_id_type=MESH)
    pl.semaphore_signal(barrier, inc=1, device_id=sibling, device_id_type=MESH)

    @pl.when(s < SECTIONS - 1)
    def _():
        pl.semaphore_signal(barrier, inc=1, device_id=nxt, device_id_type=MESH)

    @pl.when(s > 0)
    def _():
        pl.semaphore_signal(barrier, inc=1, device_id=prv, device_id_type=MESH)

    pl.semaphore_wait(barrier, CHIPS + jnp.where(first, 0, 1) + jnp.where(last, 0, 1))

    @pl.when(s > 0)
    def _():
        for j in range(NT):
            w_copy(j).wait()

    def transpose_weight():
        def body(k, _):
            kr = pl.ds(pl.multiple_of(k * TN, TN), TN)
            for j in range(NT):
                wt[j * TN : (j + 1) * TN, kr] = w[kr, j * TN : (j + 1) * TN].T
            return 0

        lax.fori_loop(0, NT, body, 0)

    def chunk_rows(m):
        return pl.ds(pl.multiple_of(m * R, R), R)

    def f_copy(m, part):
        return pltpu.make_async_remote_copy(
            src_ref=sendf.at[m, part], dst_ref=xs.at[m, part],
            send_sem=f_send.at[m], recv_sem=f_recv.at[m], device_id=nxt, device_id_type=MESH,
        )

    def b_copy(m, part):
        return pltpu.make_async_remote_copy(
            src_ref=sendb.at[m, part], dst_ref=ys.at[m, part],
            send_sem=b_send.at[m], recv_sem=b_recv.at[m], device_id=prv, device_id_type=MESH,
        )

    whole = pl.ds(0, NT)

    def sib_copy(f, m):
        rows = chunk_rows(m)
        store = ns if f == 0 else ds
        return pltpu.make_async_remote_copy(
            src_ref=store.at[rows, pl.ds(pl.multiple_of((1 - core) * BLK, BLK), BLK)], dst_ref=sib.at[f, rows, :],
            send_sem=sib_send.at[f, m], recv_sem=sib_recv.at[f, m], device_id=sibling, device_id_type=MESH,
        )

    def forward(m, send, fresh=False):
        rows = chunk_rows(m)
        total = jnp.zeros((R, TN), F32)
        for j in range(NT):
            xj = xs[m, j].astype(F32)
            total = total + xj * xj
        rinv = lax.rsqrt(jnp.sum(total, axis=-1, keepdims=True) * (1.0 / D) + 1e-06)
        rinvs[rows, :] = jnp.broadcast_to(rinv, (R, 128))
        for j in range(NT):
            cols = slice(j * TN, (j + 1) * TN)
            normed = (xs[m, j].astype(F32) * rinv * gain[:, cols]).astype(BF16)
            ns[rows, cols] = normed
            lhs[0, :R, cols] = normed
        padded = lhs[0]
        for j in range(NT):
            cols = slice(j * TN, (j + 1) * TN)
            if fresh:
                w_copy(j).wait()
            z = jnp.dot(padded, w[:, cols], preferred_element_type=F32)[:R]
            zs[rows, cols] = z
            if send:
                sendf[m, j] = (xs[m, j].astype(F32) + gelu_value(z)).astype(BF16)
                if (j + 1) % EACH == 0:
                    f_copy(m, pl.ds(j + 1 - EACH, EACH)).start()
        sib_copy(0, m).start()

    def backward(m, send):
        rows = chunk_rows(m)
        total = jnp.zeros((R, TN), F32)
        for j in range(NT):
            cols = slice(j * TN, (j + 1) * TN)
            z = zs[rows, cols]
            delta = (ys[m, j].astype(F32) * gelu_slope(z)).astype(BF16)
            ds[rows, cols] = delta
            lhs[1, :R, cols] = delta
            total = total + delta.astype(F32) * z
        if send:
            rinv = rinvs[rows, :1]
            pull = jnp.sum(total, axis=-1, keepdims=True) * (1.0 / D) * rinv
            padded = lhs[1]
            for j in range(NT):
                cols = slice(j * TN, (j + 1) * TN)
                dn = jnp.dot(padded, wt[:, cols], preferred_element_type=F32)[:R]
                xj = xs[m, j].astype(F32)
                dy = ys[m, j].astype(F32) + rinv * (dn * gain[:, cols] - xj * pull)
                sendb[m, j] = dy.astype(BF16)
                if (j + 1) % EACH == 0:
                    b_copy(m, pl.ds(j + 1 - EACH, EACH)).start()
        sib_copy(1, m).start()

    def forward_step(m):
        @pl.when(s > 0)
        def _():
            f_copy(m, whole).wait_recv()

        @pl.when(first)
        def _():
            loaded(xs, m)

        @pl.when(first & (m == 0))
        def _():
            forward(m, True, True)

        @pl.when((s < SECTIONS - 1) & ((s > 0) | (m > 0)))
        def _():
            forward(m, True)

        @pl.when(last)
        def _():
            forward(m, False)

    def backward_step(m):
        @pl.when(s < SECTIONS - 1)
        def _():
            b_copy(m, whole).wait_recv()

        @pl.when(last)
        def _():
            loaded(ys, m)

        @pl.when(s > 0)
        def _():
            backward(m, True)

        @pl.when(first)
        def _():
            backward(m, False)

    def rs_copy(f, k):
        return pltpu.make_async_remote_copy(
            src_ref=gram.at[f, pl.ds(k, KEPT), pl.ds(pl.multiple_of(k * SLAB, SLAB), SLAB), :],
            dst_ref=rs.at[f, chip],
            send_sem=rs_send.at[f, k], recv_sem=rs_recv.at[f, chip], device_id=peer(k), device_id_type=MESH,
        )

    def rs_arrival(f, k):
        return pltpu.make_async_remote_copy(
            src_ref=rs.at[f, k], dst_ref=rs.at[f, k],
            send_sem=rs_send.at[f, k], recv_sem=rs_recv.at[f, k], device_id=peer(k), device_id_type=MESH,
        )

    def ag_copy(f, k):
        return pltpu.make_async_remote_copy(
            src_ref=ag.at[f, chip], dst_ref=ag.at[f, chip],
            send_sem=ag_send.at[f, k], recv_sem=ag_recv.at[f, chip], device_id=peer(k), device_id_type=MESH,
        )

    def ag_arrival(f, k):
        return pltpu.make_async_remote_copy(
            src_ref=ag.at[f, k], dst_ref=ag.at[f, k],
            send_sem=ag_send.at[f, k], recv_sem=ag_recv.at[f, k], device_id=peer(k), device_id_type=MESH,
        )

    def each_peer(fn):
        def body(k, _):
            fn((chip + k) % CHIPS)
            return 0

        lax.fori_loop(1, CHIPS, body, 0)

    def gram_send(f):
        def landed(m, _):
            sib_copy(f, m).wait_recv()
            return 0

        lax.fori_loop(0, M, landed, 0)
        store = ns if f == 0 else ds
        mine = pl.ds(pl.multiple_of(core * BLK, BLK), BLK)
        own = store[:, mine]
        other = sib[f]
        dims = (((0,), (0,)), ((), ()))
        for q in range(BLK // 256):
            cut = slice(q * 256, (q + 1) * 256)
            own_cut = store[:, pl.ds(pl.multiple_of(core * BLK + q * 256, 256), 256)]
            part = lax.dot_general(own_cut, own, dims, preferred_element_type=F32)
            part = part + lax.dot_general(sib[f, :, cut], other, dims, preferred_element_type=F32)
            part = part.astype(BF16)
            for t in range(CHIPS):
                tile = part[:, t * SLAB : (t + 1) * SLAB]
                gram[f, t, cut, :] = tile
                if t < KEPT - 1:
                    gram[f, t + CHIPS, cut, :] = tile
        each_peer(lambda k: rs_copy(f, k).start())

    def sum_gather(f):
        mine = pl.ds(pl.multiple_of(chip * SLAB, SLAB), SLAB)
        rs[f, chip] = gram[f, pl.ds(chip, KEPT), mine, :]
        each_peer(lambda k: rs_arrival(f, k).wait_recv())
        ri = lax.broadcasted_iota(jnp.int32, (SLAB, SLAB), 0)
        ci = lax.broadcasted_iota(jnp.int32, (SLAB, SLAB), 1)
        eye = ri == ci
        for j in range(KEPT):
            total = rs[f, 0, j].astype(F32)
            for k in range(1, CHIPS):
                total = total + rs[f, k, j].astype(F32)
            total = total * (1.0 / ROW_TOTAL)
            if j == 0:
                diag = jnp.sum(jnp.where(eye, total, 0.0), axis=0, keepdims=True) + DAMPING
                high = diag.astype(BF16).astype(F32)
                row = lax.broadcasted_iota(jnp.int32, (16, SLAB), 0)
                extra = jnp.where(row == 0, high, jnp.where(row == 1, diag - high, 0.0))
                ag[f, chip, KEPT * SLAB : KEPT * SLAB + 16, :] = extra.astype(BF16)
                total = jnp.where(eye, 0.0, total)
            ag[f, chip, j * SLAB : (j + 1) * SLAB, :] = total.astype(BF16)
        each_peer(lambda k: ag_copy(f, k).start())

    def roots(f, out):
        each_peer(lambda k: ag_arrival(f, k).wait_recv())
        pieces = []
        for k in range(CHIPS):
            here = slice(k * SLAB, (k + 1) * SLAB)
            for j in range(KEPT):
                there = (k + j) % CHIPS
                there = slice(there * SLAB, (there + 1) * SLAB)
                tile = ag[f, k, j * SLAB : (j + 1) * SLAB, :]
                full[here, there] = tile
                if 0 < j < KEPT - 1:
                    full[there, here] = tile.T
            extra = ag[f, k, KEPT * SLAB : KEPT * SLAB + 16, :].astype(F32)
            pieces.append(jnp.sum(extra, axis=0, keepdims=True))
        diag = jnp.concatenate(pieces, axis=1)
        bound = jnp.abs(diag)
        for k in range(CHIPS):
            part = jnp.abs(full[k * SLAB : (k + 1) * SLAB, :].astype(F32))
            bound = bound + jnp.sum(part, axis=0, keepdims=True)
        scale = 1.0 / jnp.max(bound, axis=1, keepdims=True)
        mine = pl.ds(pl.multiple_of(chip * SLAB, SLAB), SLAB)
        ri = lax.broadcasted_iota(jnp.int32, (SLAB, BLK), 0)
        ci = lax.broadcasted_iota(jnp.int32, (SLAB, BLK), 1)
        eye = ci == ri + chip * SLAB
        scaled_diag = diag * scale
        off = full[mine, :].astype(F32) * scale
        slab[0] = off
        slab[1] = jnp.where(eye, scaled_diag, off)

        def times(u):
            u_diag = jnp.sum(jnp.where(eye, u, 0.0), axis=1, keepdims=True)
            u_off = jnp.where(eye, 0.0, u).astype(BF16)
            prod = jnp.dot(u_off, full[...], preferred_element_type=F32) * scale
            return prod + u_diag * slab[0] + u * scaled_diag

        u = times(0.0625 * slab[1]) - 0.5625 * slab[1]
        u = times(u) + 1.6875 * slab[1]
        u = times(u) - 2.4375 * slab[1]
        ztile[f] = u + jnp.where(eye, 2.25, 0.0)
        cols = pl.ds(pl.multiple_of(core * BLK, BLK), BLK)
        to_sibling(f, out).start()
        to_out(f, out).start()

    def to_sibling(f, out):
        cols = pl.ds(pl.multiple_of(core * BLK, BLK), BLK)
        return pltpu.make_async_remote_copy(
            src_ref=ztile.at[f, pl.ds(pl.multiple_of((1 - core) * HALF, HALF), HALF), :], dst_ref=out.at[:, cols],
            send_sem=out_send.at[f], recv_sem=out_recv.at[f], device_id=sibling, device_id_type=MESH,
        )

    def to_out(f, out):
        cols = pl.ds(pl.multiple_of(core * BLK, BLK), BLK)
        return pltpu.make_async_copy(
            ztile.at[f, pl.ds(pl.multiple_of(core * HALF, HALF), HALF), :], out.at[:, cols], own_sem.at[f]
        )

    @pl.when(s >= 4)
    def _():
        transpose_weight()

    lag = jnp.minimum(M, (SECTIONS - 1 - s) * LAG)

    def first_half(i, _):
        forward_step(i)

        @pl.when(i >= lag)
        def _():
            backward_step(i - lag)

        return 0

    lax.fori_loop(0, M, first_half, 0)

    @pl.when((s >= 1) & (s < 4))
    def _():
        transpose_weight()

    @pl.when(s <= 4)
    def _():
        gram_send(0)

    @pl.when(s <= 3)
    def _():
        sum_gather(0)

    @pl.when(s <= 2)
    def _():
        roots(0, act_out)

    def second_half(i, _):
        backward_step(i)
        return 0

    lax.fori_loop(M - lag, M, second_half, 0)

    @pl.when(s >= 5)
    def _():
        gram_send(0)

    gram_send(1)

    @pl.when(s >= 4)
    def _():
        sum_gather(0)

    sum_gather(1)

    @pl.when(s >= 3)
    def _():
        roots(0, act_out)

    roots(1, grad_out)

    for f, out in ((0, act_out), (1, grad_out)):
        to_out(f, out).wait()
        to_sibling(f, out).wait()

    def sent(m, _):
        @pl.when(s < SECTIONS - 1)
        def _():
            f_copy(m, whole).wait_send()

        @pl.when(s > 0)
        def _():
            b_copy(m, whole).wait_send()

        sib_copy(0, m).wait_send()
        sib_copy(1, m).wait_send()
        return 0

    lax.fori_loop(0, M, sent, 0)
    for f in range(2):
        each_peer(lambda k: rs_copy(f, k).wait_send())
        each_peer(lambda k: ag_copy(f, k).wait_send())


def copy_kernel(act, grad, act_out, grad_out):
    act_out[...] = act[...]
    grad_out[...] = grad[...]


def shards(tokens, cotangent, gain, weight):
    out = jax.ShapeDtypeStruct((HALF, D), F32)
    dma = pltpu.SemaphoreType.DMA
    anywhere = pl.BlockSpec(memory_space=pl.ANY)
    chunks = (M, R, D)
    act, grad = pl.pallas_call(
        kernel,
        out_shape=(out, out),
        in_specs=[anywhere, anywhere, pl.BlockSpec(memory_space=pltpu.VMEM), anywhere],
        out_specs=(anywhere, anywhere),
        scratch_shapes=[
            pltpu.VMEM((D, D), BF16),
            pltpu.VMEM((D, D), BF16),
            pltpu.VMEM((M, NT, R, TN), BF16),
            pltpu.VMEM((M, NT, R, TN), BF16),
            pltpu.VMEM((M, NT, R, TN), BF16),
            pltpu.VMEM((M, NT, R, TN), BF16),
            pltpu.VMEM((ROWS, D), F32),
            pltpu.VMEM((ROWS, D), BF16),
            pltpu.VMEM((ROWS, D), BF16),
            pltpu.VMEM((ROWS, 128), F32),
            pltpu.VMEM((2, ROWS, BLK), BF16),
            pltpu.VMEM((2, CHIPS + KEPT - 1, BLK, SLAB), BF16),
            pltpu.VMEM((2, CHIPS, KEPT, SLAB, SLAB), BF16),
            pltpu.VMEM((2, CHIPS, KEPT * SLAB + 16, SLAB), BF16),
            pltpu.VMEM((BLK, BLK), BF16),
            pltpu.VMEM((2, SLAB, BLK), F32),
            pltpu.VMEM((2, SLAB, BLK), F32),
            pltpu.VMEM((2, PAD, D), BF16),
            dma((NT,)),
            dma((2,)),
            dma((M,)),
            dma((M,)),
            dma((M,)),
            dma((M,)),
            dma((2, M)),
            dma((2, M)),
            dma((2, CHIPS)),
            dma((2, CHIPS)),
            dma((2, CHIPS)),
            dma((2, CHIPS)),
            dma((2,)),
            dma((2,)),
            dma((2,)),
        ],
        name="refresh",
        compiler_params=pltpu.CompilerParams(
            collective_id=0, has_side_effects=True, vmem_limit_bytes=58 * 2**20
        ),
    )(tokens.reshape(chunks), cotangent.reshape(chunks), gain, weight)
    return pl.pallas_call(
        copy_kernel,
        out_shape=(out, out),
        name="results",
    )(act, grad)


def solution(mesh):
    return jax.shard_map(
        shards,
        mesh=mesh,
        in_specs=(P(None, "dp", None), P(None, "dp", None), P("section", None), P("section", None)),
        out_specs=(P(("section", "dp"), None), P(("section", "dp"), None)),
        check_vma=False,
    )
```

```python
import functools

import jax
import jax.numpy as jnp
from jax import lax
from jax.experimental import pallas as pl
from jax.experimental.pallas import tpu as pltpu
from jax.sharding import PartitionSpec as P

MESH = pl.DeviceIdType.MESH
F32 = jnp.float32
BF16 = jnp.bfloat16

D = 2048
BLK = 1024
ROWS = 256
R = 32
M = ROWS // R
TN = 256
NT = D // TN
CHIPS = 8
SLAB = BLK // CHIPS
HALF = SLAB // 2
KEPT = 5
YZ = 3
ZY = KEPT - YZ
EXTRA = 16
SPLIT = EXTRA + YZ * SLAB
ROW_TOTAL = 4096.0
DAMPING = 4.0
SECTIONS = 8
LAG = 3
PAD = 128
EACH = 4

GELU_A = 0.7978845608028654
GELU_B = 0.044715


def gelu_value(z):
    t = jnp.tanh(GELU_A * (z + GELU_B * (z * z * z)))
    return 0.5 * z * (1.0 + t)


def gelu_slope(z):
    sq = z * z
    t = jnp.tanh(GELU_A * (z + GELU_B * (sq * z)))
    return 0.5 * (1.0 + t) + 0.5 * z * (1.0 - t * t) * (GELU_A * (1.0 + 3.0 * GELU_B * sq))


def kernel(
    tok, cot, gain, wgt, act_out, grad_out,
    w, wt, xs, ys, sendf, sendb, zs, ns, ds, rinvs, sib, gram, yp, zq, ps, qs, zp, yq, ag, full, dv, slab, ztile, lhs,
    w_sem, tok_sem, f_send, f_recv, b_send, b_recv, sib_send, sib_recv,
    yp_send, yp_recv, zq_send, zq_recv, zp_send, zp_recv, yq_send, yq_recv,
    gp_zsend, gp_ysend, gp_recv, gq_ysend, gq_zsend, gq_fsend, gq_recv, cot_send, own_sem, out_send, out_recv,
):
    s = lax.axis_index("section")
    d = lax.axis_index("dp")
    chip = d // 2
    core = d % 2
    zc = d // 4
    yc = (d // 2) % 2
    flipped = zc * 4 + (1 - yc) * 2 + core
    nxt = (jnp.minimum(s + 1, SECTIONS - 1), jnp.where(s == 3, flipped, d))
    prv = (jnp.maximum(s - 1, 0), jnp.where(s == 4, flipped, d))
    ypeer = (s, flipped)
    sibling = (s, chip * 2 + 1 - core)
    first = s == 0
    last = s == SECTIONS - 1

    def zpeer(z):
        return (s, z * 4 + yc * 2 + core)

    def remote(src, dst, send_sem, recv_sem, device):
        return pltpu.make_async_remote_copy(
            src_ref=src, dst_ref=dst, send_sem=send_sem, recv_sem=recv_sem, device_id=device, device_id_type=MESH
        )

    def w_copy(j):
        cols = pl.ds(j * TN, TN)
        return pltpu.make_async_copy(wgt.at[:, cols], w.at[:, cols], w_sem.at[j])

    def first_load(source, target, j):
        cols = pl.ds(j * TN, TN)
        return pltpu.make_async_copy(source.at[0, :, cols], target.at[0, j], tok_sem.at[0])

    def cot_copy(part, j):
        cols = pl.ds(j * TN, TN)
        chunk = 0 if part == 0 else slice(1, M)
        return remote(cot.at[chunk, :, cols], ys.at[chunk, j], cot_send.at[part], tok_sem.at[part], ypeer)

    def cot_whole(part):
        chunk = ys.at[0] if part == 0 else ys.at[1:M]
        return remote(chunk, chunk, cot_send.at[part], tok_sem.at[part], ypeer)

    def rest_load(source, target, j):
        cols = pl.ds(j * TN, TN)
        return pltpu.make_async_copy(source.at[1:M, :, cols], target.at[1:M, j], tok_sem.at[1])

    def loaded(target, m):
        @pl.when(m == 0)
        def _():
            pltpu.make_async_copy(target.at[0], target.at[0], tok_sem.at[0]).wait()

        @pl.when(m == 1)
        def _():
            pltpu.make_async_copy(target.at[1:M], target.at[1:M], tok_sem.at[1]).wait()

    @pl.when(first)
    def _():
        for j in range(NT):
            first_load(tok, xs, j).start()

    for j in range(NT):
        w_copy(j).start()

    @pl.when(first)
    def _():
        for j in range(NT):
            rest_load(tok, xs, j).start()

    lhs[...] = jnp.zeros_like(lhs)

    barrier = pltpu.get_barrier_semaphore()
    for neighbour in [sibling, ypeer] + [zpeer((zc + i) % 4) for i in range(1, 4)]:
        pl.semaphore_signal(barrier, inc=1, device_id=neighbour, device_id_type=MESH)

    @pl.when(s < SECTIONS - 1)
    def _():
        pl.semaphore_signal(barrier, inc=1, device_id=nxt, device_id_type=MESH)

    @pl.when(s > 0)
    def _():
        pl.semaphore_signal(barrier, inc=1, device_id=prv, device_id_type=MESH)

    pl.semaphore_wait(barrier, 5 + jnp.where(first, 0, 1) + jnp.where(last, 0, 1))

    @pl.when(last)
    def _():
        for j in range(NT):
            cot_copy(0, j).start()
        for j in range(NT):
            cot_copy(1, j).start()

    @pl.when(s > 0)
    def _():
        for j in range(NT):
            w_copy(j).wait()

    def transpose_weight():
        def body(k, _):
            kr = pl.ds(pl.multiple_of(k * TN, TN), TN)
            for j in range(NT):
                wt[j * TN : (j + 1) * TN, kr] = w[kr, j * TN : (j + 1) * TN].T
            return 0

        lax.fori_loop(0, NT, body, 0)

    def chunk_rows(m):
        return pl.ds(pl.multiple_of(m * R, R), R)

    def f_copy(m, part):
        return pltpu.make_async_remote_copy(
            src_ref=sendf.at[m, part], dst_ref=xs.at[m, part],
            send_sem=f_send.at[m], recv_sem=f_recv.at[m], device_id=nxt, device_id_type=MESH,
        )

    def b_copy(m, part):
        return pltpu.make_async_remote_copy(
            src_ref=sendb.at[m, part], dst_ref=ys.at[m, part],
            send_sem=b_send.at[m], recv_sem=b_recv.at[m], device_id=prv, device_id_type=MESH,
        )

    whole = pl.ds(0, NT)

    def sib_copy(f, m):
        rows = chunk_rows(m)
        store = ns if f == 0 else ds
        return pltpu.make_async_remote_copy(
            src_ref=store.at[rows, pl.ds(pl.multiple_of((1 - core) * BLK, BLK), BLK)], dst_ref=sib.at[f, rows, :],
            send_sem=sib_send.at[f, m], recv_sem=sib_recv.at[f, m], device_id=sibling, device_id_type=MESH,
        )

    def forward(m, send, fresh=False):
        rows = chunk_rows(m)
        total = jnp.zeros((R, TN), F32)
        for j in range(NT):
            xj = xs[m, j].astype(F32)
            total = total + xj * xj
        rinv = lax.rsqrt(jnp.sum(total, axis=-1, keepdims=True) * (1.0 / D) + 1e-06)
        rinvs[rows, :] = jnp.broadcast_to(rinv, (R, 128))
        for j in range(NT):
            cols = slice(j * TN, (j + 1) * TN)
            normed = (xs[m, j].astype(F32) * rinv * gain[:, cols]).astype(BF16)
            ns[rows, cols] = normed
            lhs[0, :R, cols] = normed
        padded = lhs[0]
        for j in range(NT):
            cols = slice(j * TN, (j + 1) * TN)
            if fresh:
                w_copy(j).wait()
            z = jnp.dot(padded, w[:, cols], preferred_element_type=F32)[:R]
            zs[rows, cols] = z
            if send:
                sendf[m, j] = (xs[m, j].astype(F32) + gelu_value(z)).astype(BF16)
                if (j + 1) % EACH == 0:
                    f_copy(m, pl.ds(j + 1 - EACH, EACH)).start()
        sib_copy(0, m).start()

    def backward(m, send):
        rows = chunk_rows(m)
        total = jnp.zeros((R, TN), F32)
        for j in range(NT):
            cols = slice(j * TN, (j + 1) * TN)
            z = zs[rows, cols]
            delta = (ys[m, j].astype(F32) * gelu_slope(z)).astype(BF16)
            ds[rows, cols] = delta
            lhs[1, :R, cols] = delta
            total = total + delta.astype(F32) * z
        if send:
            rinv = rinvs[rows, :1]
            pull = jnp.sum(total, axis=-1, keepdims=True) * (1.0 / D) * rinv
            padded = lhs[1]
            for j in range(NT):
                cols = slice(j * TN, (j + 1) * TN)
                dn = jnp.dot(padded, wt[:, cols], preferred_element_type=F32)[:R]
                xj = xs[m, j].astype(F32)
                dy = ys[m, j].astype(F32) + rinv * (dn * gain[:, cols] - xj * pull)
                sendb[m, j] = dy.astype(BF16)
                if (j + 1) % EACH == 0:
                    b_copy(m, pl.ds(j + 1 - EACH, EACH)).start()
        sib_copy(1, m).start()

    def forward_step(m):
        @pl.when(s > 0)
        def _():
            f_copy(m, whole).wait_recv()

        @pl.when(first)
        def _():
            loaded(xs, m)

        @pl.when(first & (m == 0))
        def _():
            forward(m, True, True)

        @pl.when((s < SECTIONS - 1) & ((s > 0) | (m > 0)))
        def _():
            forward(m, True)

        @pl.when(last)
        def _():
            forward(m, False)

    def backward_step(m):
        @pl.when(s < SECTIONS - 1)
        def _():
            b_copy(m, whole).wait_recv()

        @pl.when(last & (m == 0))
        def _():
            cot_whole(0).wait_recv()

        @pl.when(last & (m == 1))
        def _():
            cot_whole(1).wait_recv()

        @pl.when(s > 0)
        def _():
            backward(m, True)

        @pl.when(first)
        def _():
            backward(m, False)

    def slab_of(f, k, tile, count):
        return gram.at[f, pl.ds(k + tile, count), pl.ds(pl.multiple_of(k * SLAB, SLAB), SLAB), :]

    def yp_copy(f, z):
        src = slab_of(f, 2 * z + 1 - yc, 0, YZ)
        return remote(src, yp.at[f, z], yp_send.at[f, z], yp_recv.at[f, z], ypeer)

    def zq_copy(f, z, y):
        src = slab_of(f, 2 * z + y, YZ, ZY)
        return remote(src, zq.at[f, zc, y], zq_send.at[f, z, y], zq_recv.at[f, zc, y], zpeer(z))

    def zq_arrival(f, z, y):
        return remote(zq.at[f, z, y], zq.at[f, z, y], zq_send.at[f, z, y], zq_recv.at[f, z, y], zpeer(z))

    def zp_copy(f, z):
        return remote(ps.at[f, z], zp.at[f, zc], zp_send.at[f, z], zp_recv.at[f, zc], zpeer(z))

    def zp_arrival(f, z):
        return remote(zp.at[f, z], zp.at[f, z], zp_send.at[f, z], zp_recv.at[f, z], zpeer(z))

    def yq_copy(f):
        return remote(qs.at[f], yq.at[f], yq_send.at[f], yq_recv.at[f], ypeer)

    def gp_copy(f, k, send_sem, device):
        part = ag.at[f, k, pl.ds(0, SPLIT), :]
        return remote(part, part, send_sem, gp_recv.at[f, k], device)

    def gq_copy(f, k, send_sem, device):
        part = ag.at[f, k, pl.ds(SPLIT, ZY * SLAB), :]
        return remote(part, part, send_sem, gq_recv.at[f, k], device)

    def gp_z(f, z):
        return gp_copy(f, chip, gp_zsend.at[f, z], zpeer(z))

    def gp_y(f, z):
        return gp_copy(f, 2 * z + yc, gp_ysend.at[f, z], ypeer)

    def gq_y(f):
        return gq_copy(f, chip, gq_ysend.at[f], ypeer)

    def gq_z(f, z):
        return gq_copy(f, chip, gq_zsend.at[f, z], zpeer(z))

    def gq_f(f, z):
        return gq_copy(f, 2 * zc + 1 - yc, gq_fsend.at[f, z], zpeer(z))

    def other_z(fn):
        def body(i, _):
            fn((zc + i) % 4)
            return 0

        lax.fori_loop(1, 4, body, 0)

    def gram_send(f):
        def landed(m, _):
            sib_copy(f, m).wait_recv()
            return 0

        lax.fori_loop(0, M, landed, 0)
        store = ns if f == 0 else ds
        mine = pl.ds(pl.multiple_of(core * BLK, BLK), BLK)
        own = store[:, mine]
        other = sib[f]
        dims = (((0,), (0,)), ((), ()))
        for q in range(BLK // 256):
            cut = slice(q * 256, (q + 1) * 256)
            own_cut = store[:, pl.ds(pl.multiple_of(core * BLK + q * 256, 256), 256)]
            part = lax.dot_general(own_cut, own, dims, preferred_element_type=F32)
            part = part + lax.dot_general(sib[f, :, cut], other, dims, preferred_element_type=F32)
            part = part.astype(BF16)
            for t in range(CHIPS):
                tile = part[:, t * SLAB : (t + 1) * SLAB]
                gram[f, t, cut, :] = tile
                if t < KEPT - 1:
                    gram[f, t + CHIPS, cut, :] = tile
            yp_copy(f, q).start()

            @pl.when(zc != q)
            def _():
                for y in range(2):
                    zq_copy(f, q, y).start()

    def mine_tile(f, k, t):
        return gram[f, k + t, pl.ds(pl.multiple_of(k * SLAB, SLAB), SLAB), :].astype(F32)

    def sum_gather(f):
        def relay(z):
            yp_copy(f, z).wait_recv()
            for t in range(YZ):
                ps[f, z, t] = (mine_tile(f, 2 * z + yc, t) + yp[f, z, t].astype(F32)).astype(BF16)
            zp_copy(f, z).start()

        other_z(relay)
        other_z(lambda z: zq_arrival(f, z, 1 - yc).wait_recv())
        for t in range(ZY):
            total = mine_tile(f, 2 * zc + 1 - yc, YZ + t)
            for i in range(1, 4):
                total = total + zq[f, (zc + i) % 4, 1 - yc, t].astype(F32)
            qs[f, t] = total.astype(BF16)
        yq_copy(f).start()
        yp_copy(f, zc).wait_recv()
        other_z(lambda z: zq_arrival(f, z, yc).wait_recv())
        other_z(lambda z: zp_arrival(f, z).wait_recv())
        ri = lax.broadcasted_iota(jnp.int32, (SLAB, SLAB), 0)
        ci = lax.broadcasted_iota(jnp.int32, (SLAB, SLAB), 1)
        eye = ri == ci

        def put(t, total):
            ag[f, chip, EXTRA + t * SLAB : EXTRA + (t + 1) * SLAB, :] = total.astype(BF16)

        for t in range(YZ):
            total = mine_tile(f, chip, t) + yp[f, zc, t].astype(F32)
            for i in range(1, 4):
                total = total + zp[f, (zc + i) % 4, t].astype(F32)
            total = total * (1.0 / ROW_TOTAL)
            if t == 0:
                diag = jnp.sum(jnp.where(eye, total, 0.0), axis=0, keepdims=True) + DAMPING
                high = diag.astype(BF16).astype(F32)
                row = lax.broadcasted_iota(jnp.int32, (EXTRA, SLAB), 0)
                extra = jnp.where(row == 0, high, jnp.where(row == 1, diag - high, 0.0))
                ag[f, chip, 0:EXTRA, :] = extra.astype(BF16)
                total = jnp.where(eye, 0.0, total)
            put(t, total)
        other_z(lambda z: gp_z(f, z).start())
        gp_y(f, zc).start()
        yq_copy(f).wait_recv()
        for t in range(ZY):
            total = mine_tile(f, chip, YZ + t) + yq[f, t].astype(F32)
            for i in range(1, 4):
                total = total + zq[f, (zc + i) % 4, yc, t].astype(F32)
            put(YZ + t, total * (1.0 / ROW_TOTAL))
        gq_y(f).start()
        other_z(lambda z: gq_z(f, z).start())

    def assemble(f, k):
        here = pl.ds(pl.multiple_of(k * SLAB, SLAB), SLAB)
        for j in range(KEPT):
            there = pl.ds(pl.multiple_of(((k + j) % CHIPS) * SLAB, SLAB), SLAB)
            tile = ag[f, k, EXTRA + j * SLAB : EXTRA + (j + 1) * SLAB, :]
            full[here, there] = tile
            if 0 < j < KEPT - 1:
                full[there, here] = tile.T
        dv[:, here] = jnp.sum(ag[f, k, 0:EXTRA, :].astype(F32), axis=0, keepdims=True)

    def gathered(f, k):
        gp_copy(f, k, gp_ysend.at[f, 0], ypeer).wait_recv()
        gq_copy(f, k, gq_ysend.at[f], ypeer).wait_recv()

    def roots(f, out):
        across = 2 * zc + 1 - yc

        def pass_on(z):
            gp_copy(f, 2 * z + yc, gp_ysend.at[f, z], ypeer).wait_recv()
            gp_y(f, z).start()

        pass_on((zc + 1) % 4)
        gathered(f, across)
        other_z(lambda z: gq_f(f, z).start())
        pass_on((zc + 3) % 4)
        pass_on((zc + 2) % 4)
        assemble(f, chip)
        assemble(f, across)

        def direct(z):
            gq_copy(f, 2 * z + yc, gq_ysend.at[f], ypeer).wait_recv()
            assemble(f, 2 * z + yc)

        def indirect(z):
            gathered(f, 2 * z + 1 - yc)
            assemble(f, 2 * z + 1 - yc)

        other_z(direct)
        other_z(indirect)
        diag = dv[...]
        ones = jnp.ones((16, BLK), BF16)
        bound = jnp.abs(diag) + jnp.dot(ones, jnp.abs(full[...]), preferred_element_type=F32)[:1]
        scale = 1.0 / jnp.max(bound, axis=1, keepdims=True)
        mine = pl.ds(pl.multiple_of(chip * SLAB, SLAB), SLAB)
        ri = lax.broadcasted_iota(jnp.int32, (SLAB, BLK), 0)
        ci = lax.broadcasted_iota(jnp.int32, (SLAB, BLK), 1)
        eye = ci == ri + chip * SLAB
        scaled_diag = diag * scale
        off = full[mine, :].astype(F32) * scale
        slab[0] = off
        slab[1] = jnp.where(eye, scaled_diag, off)

        def times(u):
            u_diag = jnp.sum(jnp.where(eye, u, 0.0), axis=1, keepdims=True)
            u_off = jnp.where(eye, 0.0, u).astype(BF16)
            prod = jnp.dot(u_off, full[...], preferred_element_type=F32) * scale
            return prod + u_diag * slab[0] + u * scaled_diag

        u = times(0.0625 * slab[1]) - 0.5625 * slab[1]
        u = times(u) + 1.6875 * slab[1]
        u = times(u) - 2.4375 * slab[1]
        ztile[f] = u + jnp.where(eye, 2.25, 0.0)
        cols = pl.ds(pl.multiple_of(core * BLK, BLK), BLK)
        to_sibling(f, out).start()
        to_out(f, out).start()

    def to_sibling(f, out):
        cols = pl.ds(pl.multiple_of(core * BLK, BLK), BLK)
        return pltpu.make_async_remote_copy(
            src_ref=ztile.at[f, pl.ds(pl.multiple_of((1 - core) * HALF, HALF), HALF), :], dst_ref=out.at[:, cols],
            send_sem=out_send.at[f], recv_sem=out_recv.at[f], device_id=sibling, device_id_type=MESH,
        )

    def to_out(f, out):
        cols = pl.ds(pl.multiple_of(core * BLK, BLK), BLK)
        return pltpu.make_async_copy(
            ztile.at[f, pl.ds(pl.multiple_of(core * HALF, HALF), HALF), :], out.at[:, cols], own_sem.at[f]
        )

    @pl.when(s >= 4)
    def _():
        transpose_weight()

    lag = jnp.minimum(M, (SECTIONS - 1 - s) * LAG)

    def first_half(i, _):
        forward_step(i)

        @pl.when(i >= lag)
        def _():
            backward_step(i - lag)

        return 0

    lax.fori_loop(0, M, first_half, 0)

    @pl.when((s >= 1) & (s < 4))
    def _():
        transpose_weight()

    @pl.when(s <= 4)
    def _():
        gram_send(0)

    @pl.when(s <= 3)
    def _():
        sum_gather(0)

    @pl.when(s <= 2)
    def _():
        roots(0, act_out)

    def second_half(i, _):
        backward_step(i)
        return 0

    lax.fori_loop(M - lag, M, second_half, 0)

    @pl.when(s >= 5)
    def _():
        gram_send(0)

    gram_send(1)

    @pl.when(s >= 4)
    def _():
        sum_gather(0)

    sum_gather(1)

    @pl.when(s >= 3)
    def _():
        roots(0, act_out)

    roots(1, grad_out)

    for f, out in ((0, act_out), (1, grad_out)):
        to_out(f, out).wait()
        to_sibling(f, out).wait()

    def sent(m, _):
        @pl.when(s < SECTIONS - 1)
        def _():
            f_copy(m, whole).wait_send()

        @pl.when(s > 0)
        def _():
            b_copy(m, whole).wait_send()

        sib_copy(0, m).wait_send()
        sib_copy(1, m).wait_send()
        return 0

    lax.fori_loop(0, M, sent, 0)
    @pl.when(last)
    def _():
        cot_whole(0).wait_send()
        cot_whole(1).wait_send()

    for f in range(2):

        def z_sent(z):
            zq_copy(f, z, 0).wait_send()
            zq_copy(f, z, 1).wait_send()
            zp_copy(f, z).wait_send()
            gp_z(f, z).wait_send()
            gp_y(f, z).wait_send()
            yp_copy(f, z).wait_send()
            gq_z(f, z).wait_send()
            gq_f(f, z).wait_send()

        other_z(z_sent)
        yp_copy(f, zc).wait_send()
        gp_y(f, zc).wait_send()
        yq_copy(f).wait_send()
        gq_y(f).wait_send()


def copy_kernel(act, grad, act_out, grad_out):
    act_out[...] = act[...]
    grad_out[...] = grad[...]


def shards(tokens, cotangent, gain, weight):
    out = jax.ShapeDtypeStruct((HALF, D), F32)
    dma = pltpu.SemaphoreType.DMA
    anywhere = pl.BlockSpec(memory_space=pl.ANY)
    chunks = (M, R, D)
    act, grad = pl.pallas_call(
        kernel,
        out_shape=(out, out),
        in_specs=[anywhere, anywhere, pl.BlockSpec(memory_space=pltpu.VMEM), anywhere],
        out_specs=(anywhere, anywhere),
        scratch_shapes=[
            pltpu.VMEM((D, D), BF16),
            pltpu.VMEM((D, D), BF16),
            pltpu.VMEM((M, NT, R, TN), BF16),
            pltpu.VMEM((M, NT, R, TN), BF16),
            pltpu.VMEM((M, NT, R, TN), BF16),
            pltpu.VMEM((M, NT, R, TN), BF16),
            pltpu.VMEM((ROWS, D), F32),
            pltpu.VMEM((ROWS, D), BF16),
            pltpu.VMEM((ROWS, D), BF16),
            pltpu.VMEM((ROWS, 128), F32),
            pltpu.VMEM((2, ROWS, BLK), BF16),
            pltpu.VMEM((2, CHIPS + KEPT - 1, BLK, SLAB), BF16),
            pltpu.VMEM((2, 4, YZ, SLAB, SLAB), BF16),
            pltpu.VMEM((2, 4, 2, ZY, SLAB, SLAB), BF16),
            pltpu.VMEM((2, 4, YZ, SLAB, SLAB), BF16),
            pltpu.VMEM((2, ZY, SLAB, SLAB), BF16),
            pltpu.VMEM((2, 4, YZ, SLAB, SLAB), BF16),
            pltpu.VMEM((2, ZY, SLAB, SLAB), BF16),
            pltpu.VMEM((2, CHIPS, EXTRA + KEPT * SLAB, SLAB), BF16),
            pltpu.VMEM((BLK, BLK), BF16),
            pltpu.VMEM((1, BLK), F32),
            pltpu.VMEM((2, SLAB, BLK), F32),
            pltpu.VMEM((2, SLAB, BLK), F32),
            pltpu.VMEM((2, PAD, D), BF16),
            dma((NT,)),
            dma((2,)),
            dma((M,)),
            dma((M,)),
            dma((M,)),
            dma((M,)),
            dma((2, M)),
            dma((2, M)),
            dma((2, 4)),
            dma((2, 4)),
            dma((2, 4, 2)),
            dma((2, 4, 2)),
            dma((2, 4)),
            dma((2, 4)),
            dma((2,)),
            dma((2,)),
            dma((2, 4)),
            dma((2, 4)),
            dma((2, CHIPS)),
            dma((2,)),
            dma((2, 4)),
            dma((2, 4)),
            dma((2, CHIPS)),
            dma((2,)),
            dma((2,)),
            dma((2,)),
            dma((2,)),
        ],
        name="refresh",
        compiler_params=pltpu.CompilerParams(
            collective_id=0, has_side_effects=True, vmem_limit_bytes=58 * 2**20
        ),
    )(tokens.reshape(chunks), cotangent.reshape(chunks), gain, weight)
    return pl.pallas_call(
        copy_kernel,
        out_shape=(out, out),
        name="results",
    )(act, grad)


def solution(mesh):
    return jax.shard_map(
        shards,
        mesh=mesh,
        in_specs=(P(None, "dp", None), P(None, "dp", None), P("section", None), P("section", None)),
        out_specs=(P(("section", "dp"), None), P(("section", "dp"), None)),
        check_vma=False,
    )
```

```python
import functools

import jax
import jax.numpy as jnp
from jax import lax
from jax.experimental import pallas as pl
from jax.experimental.pallas import tpu as pltpu
from jax.sharding import PartitionSpec as P

MESH = pl.DeviceIdType.MESH
F32 = jnp.float32
BF16 = jnp.bfloat16

D = 2048
BLK = 1024
ROWS = 256
R = 32
M = ROWS // R
TN = 256
NT = D // TN
CHIPS = 8
SLAB = BLK // CHIPS
HALF = SLAB // 2
KEPT = 5
YZ = 2
ZY = KEPT - YZ
EXTRA = 16
SPLIT = EXTRA + YZ * SLAB
ROW_TOTAL = 4096.0
DAMPING = 4.0
SECTIONS = 8
LAG = 3
PAD = 128
GROUPS = ((0, 4, 2), (4, 8, 2))

GELU_A = 0.7978845608028654
GELU_B = 0.044715


def gelu_value(z):
    t = jnp.tanh(GELU_A * (z + GELU_B * (z * z * z)))
    return 0.5 * z * (1.0 + t)


def gelu_slope(z):
    sq = z * z
    t = jnp.tanh(GELU_A * (z + GELU_B * (sq * z)))
    return 0.5 * (1.0 + t) + 0.5 * z * (1.0 - t * t) * (GELU_A * (1.0 + 3.0 * GELU_B * sq))


def kernel(
    tok, cot, gain, wgt, act_out, grad_out,
    w, wt, xs, ys, sendf, sendb, zs, slopes, ns, ds, rinvs, sib, gram, yp, zq, ps, qs, zp, yq, ag, full, dv, slab, ztile, lhs,
    w_sem, tok_sem, f_send, f_recv, b_send, b_recv, sib_send, sib_recv,
    yp_send, yp_recv, zq_send, zq_recv, zp_send, zp_recv, yq_send, yq_recv,
    gp_zsend, gp_ysend, gp_recv, gq_ysend, gq_zsend, gq_fsend, gq_recv, cot_send, own_sem, out_send, out_recv,
):
    s = lax.axis_index("section")
    d = lax.axis_index("dp")
    chip = d // 2
    core = d % 2
    zc = d // 4
    yc = (d // 2) % 2
    flipped = zc * 4 + (1 - yc) * 2 + core
    nxt = (jnp.minimum(s + 1, SECTIONS - 1), jnp.where(s == 3, flipped, d))
    prv = (jnp.maximum(s - 1, 0), jnp.where(s == 4, flipped, d))
    ypeer = (s, flipped)
    sibling = (s, chip * 2 + 1 - core)
    first = s == 0
    last = s == SECTIONS - 1

    def zpeer(z):
        return (s, z * 4 + yc * 2 + core)

    def remote(src, dst, send_sem, recv_sem, device):
        return pltpu.make_async_remote_copy(
            src_ref=src, dst_ref=dst, send_sem=send_sem, recv_sem=recv_sem, device_id=device, device_id_type=MESH
        )

    def w_copy(j):
        cols = pl.ds(j * TN, TN)
        return pltpu.make_async_copy(wgt.at[:, cols], w.at[:, cols], w_sem.at[j])

    def first_load(source, target, j):
        cols = pl.ds(j * TN, TN)
        return pltpu.make_async_copy(source.at[0, :, cols], target.at[0, j], tok_sem.at[0])

    def cot_copy(part, j):
        cols = pl.ds(j * TN, TN)
        chunk = 0 if part == 0 else slice(1, M)
        return remote(cot.at[chunk, :, cols], ys.at[chunk, j], cot_send.at[part], tok_sem.at[part], ypeer)

    def cot_whole(part):
        chunk = ys.at[0] if part == 0 else ys.at[1:M]
        return remote(chunk, chunk, cot_send.at[part], tok_sem.at[part], ypeer)

    def rest_load(source, target, j):
        cols = pl.ds(j * TN, TN)
        return pltpu.make_async_copy(source.at[1:M, :, cols], target.at[1:M, j], tok_sem.at[1])

    def loaded(target, m):
        @pl.when(m == 0)
        def _():
            pltpu.make_async_copy(target.at[0], target.at[0], tok_sem.at[0]).wait()

        @pl.when(m == 1)
        def _():
            pltpu.make_async_copy(target.at[1:M], target.at[1:M], tok_sem.at[1]).wait()

    @pl.when(first)
    def _():
        for j in range(NT):
            first_load(tok, xs, j).start()

    for j in range(NT):
        w_copy(j).start()

    @pl.when(first)
    def _():
        for j in range(NT):
            rest_load(tok, xs, j).start()

    lhs[...] = jnp.zeros_like(lhs)

    barrier = pltpu.get_barrier_semaphore()
    for neighbour in [sibling, ypeer] + [zpeer((zc + i) % 4) for i in range(1, 4)]:
        pl.semaphore_signal(barrier, inc=1, device_id=neighbour, device_id_type=MESH)

    @pl.when(s < SECTIONS - 1)
    def _():
        pl.semaphore_signal(barrier, inc=1, device_id=nxt, device_id_type=MESH)

    @pl.when(s > 0)
    def _():
        pl.semaphore_signal(barrier, inc=1, device_id=prv, device_id_type=MESH)

    pl.semaphore_wait(barrier, 5 + jnp.where(first, 0, 1) + jnp.where(last, 0, 1))

    @pl.when(last)
    def _():
        for j in range(NT):
            cot_copy(0, j).start()
        for j in range(NT):
            cot_copy(1, j).start()

    @pl.when(s > 0)
    def _():
        for j in range(NT):
            w_copy(j).wait()

    def transpose_weight():
        def body(k, _):
            kr = pl.ds(pl.multiple_of(k * TN, TN), TN)
            for j in range(NT):
                wt[j * TN : (j + 1) * TN, kr] = w[kr, j * TN : (j + 1) * TN].T
            return 0

        lax.fori_loop(0, NT, body, 0)

    def chunk_rows(m):
        return pl.ds(pl.multiple_of(m * R, R), R)

    def f_copy(m, part):
        return pltpu.make_async_remote_copy(
            src_ref=sendf.at[m, part], dst_ref=xs.at[m, part],
            send_sem=f_send.at[m], recv_sem=f_recv.at[m], device_id=nxt, device_id_type=MESH,
        )

    def b_copy(m, part):
        return pltpu.make_async_remote_copy(
            src_ref=sendb.at[m, part], dst_ref=ys.at[m, part],
            send_sem=b_send.at[m], recv_sem=b_recv.at[m], device_id=prv, device_id_type=MESH,
        )

    whole = pl.ds(0, NT)

    def sib_copy(f, m):
        rows = chunk_rows(m)
        store = ns if f == 0 else ds
        return pltpu.make_async_remote_copy(
            src_ref=store.at[rows, pl.ds(pl.multiple_of((1 - core) * BLK, BLK), BLK)], dst_ref=sib.at[f, rows, :],
            send_sem=sib_send.at[f, m], recv_sem=sib_recv.at[f, m], device_id=sibling, device_id_type=MESH,
        )

    def forward(m, send, fresh=False):
        rows = chunk_rows(m)
        total = jnp.zeros((R, TN), F32)
        for j in range(NT):
            xj = xs[m, j].astype(F32)
            total = total + xj * xj
        rinv = lax.rsqrt(jnp.sum(total, axis=-1, keepdims=True) * (1.0 / D) + 1e-06)
        rinvs[rows, :] = jnp.broadcast_to(rinv, (R, 128))
        for j in range(NT):
            cols = slice(j * TN, (j + 1) * TN)
            normed = (xs[m, j].astype(F32) * rinv * gain[:, cols]).astype(BF16)
            ns[rows, cols] = normed
            lhs[0, :R, cols] = normed
        padded = lhs[0]
        for j in range(NT):
            cols = slice(j * TN, (j + 1) * TN)
            if fresh:
                w_copy(j).wait()
            z = jnp.dot(padded, w[:, cols], preferred_element_type=F32)[:R]
            zs[rows, cols] = z
            if send:
                sendf[m, j] = (xs[m, j].astype(F32) + gelu_value(z)).astype(BF16)
                for lo, hi, step in GROUPS:
                    if j + 1 == hi:
                        for part in range(lo, hi, step):
                            f_copy(m, pl.ds(part, step)).start()
        sib_copy(0, m).start()
        for j in range(NT):
            cols = slice(j * TN, (j + 1) * TN)
            slopes[rows, cols] = gelu_slope(zs[rows, cols])

    def backward(m, send):
        rows = chunk_rows(m)
        total = jnp.zeros((R, TN), F32)
        for j in range(NT):
            cols = slice(j * TN, (j + 1) * TN)
            z = zs[rows, cols]
            delta = (ys[m, j].astype(F32) * slopes[rows, cols]).astype(BF16)
            ds[rows, cols] = delta
            lhs[1, :R, cols] = delta
            total = total + delta.astype(F32) * z
        if send:
            rinv = rinvs[rows, :1]
            pull = jnp.sum(total, axis=-1, keepdims=True) * (1.0 / D) * rinv
            padded = lhs[1]
            for j in range(NT):
                cols = slice(j * TN, (j + 1) * TN)
                dn = jnp.dot(padded, wt[:, cols], preferred_element_type=F32)[:R]
                xj = xs[m, j].astype(F32)
                dy = ys[m, j].astype(F32) + rinv * (dn * gain[:, cols] - xj * pull)
                sendb[m, j] = dy.astype(BF16)
                for lo, hi, step in GROUPS:
                    if j + 1 == hi:
                        for part in range(lo, hi, step):
                            b_copy(m, pl.ds(part, step)).start()
        sib_copy(1, m).start()

    def forward_step(m):
        @pl.when(s > 0)
        def _():
            f_copy(m, whole).wait_recv()

        @pl.when(first)
        def _():
            loaded(xs, m)

        @pl.when(first & (m == 0))
        def _():
            forward(m, True, True)

        @pl.when((s < SECTIONS - 1) & ((s > 0) | (m > 0)))
        def _():
            forward(m, True)

        @pl.when(last)
        def _():
            forward(m, False)

    def backward_step(m):
        @pl.when(s < SECTIONS - 1)
        def _():
            b_copy(m, whole).wait_recv()

        @pl.when(last & (m == 0))
        def _():
            cot_whole(0).wait_recv()

        @pl.when(last & (m == 1))
        def _():
            cot_whole(1).wait_recv()

        @pl.when(s > 0)
        def _():
            backward(m, True)

        @pl.when(first)
        def _():
            backward(m, False)

    def slab_of(f, k, tile, count):
        return gram.at[f, pl.ds(k + tile, count), pl.ds(pl.multiple_of(k * SLAB, SLAB), SLAB), :]

    def yp_copy(f, z):
        src = slab_of(f, 2 * z + 1 - yc, 0, YZ)
        return remote(src, yp.at[f, z], yp_send.at[f, z], yp_recv.at[f, z], ypeer)

    def zq_copy(f, z, y):
        src = slab_of(f, 2 * z + y, YZ, ZY)
        return remote(src, zq.at[f, zc, y], zq_send.at[f, z, y], zq_recv.at[f, zc, y], zpeer(z))

    def zq_arrival(f, z, y):
        return remote(zq.at[f, z, y], zq.at[f, z, y], zq_send.at[f, z, y], zq_recv.at[f, z, y], zpeer(z))

    def zp_copy(f, z):
        return remote(ps.at[f, z], zp.at[f, zc], zp_send.at[f, z], zp_recv.at[f, zc], zpeer(z))

    def zp_arrival(f, z):
        return remote(zp.at[f, z], zp.at[f, z], zp_send.at[f, z], zp_recv.at[f, z], zpeer(z))

    def yq_copy(f):
        return remote(qs.at[f], yq.at[f], yq_send.at[f], yq_recv.at[f], ypeer)

    def gp_copy(f, k, send_sem, device):
        part = ag.at[f, k, pl.ds(0, SPLIT), :]
        return remote(part, part, send_sem, gp_recv.at[f, k], device)

    def gq_copy(f, k, send_sem, device):
        part = ag.at[f, k, pl.ds(SPLIT, ZY * SLAB), :]
        return remote(part, part, send_sem, gq_recv.at[f, k], device)

    def gp_z(f, z):
        return gp_copy(f, chip, gp_zsend.at[f, z], zpeer(z))

    def gp_y(f, z):
        return gp_copy(f, 2 * z + yc, gp_ysend.at[f, z], ypeer)

    def gq_y(f):
        return gq_copy(f, chip, gq_ysend.at[f], ypeer)

    def gq_z(f, z):
        return gq_copy(f, chip, gq_zsend.at[f, z], zpeer(z))

    def gq_f(f, z):
        return gq_copy(f, 2 * zc + 1 - yc, gq_fsend.at[f, z], zpeer(z))

    def other_z(fn):
        def body(i, _):
            fn((zc + i) % 4)
            return 0

        lax.fori_loop(1, 4, body, 0)

    def gram_send(f):
        def landed(m, _):
            sib_copy(f, m).wait_recv()
            return 0

        lax.fori_loop(0, M, landed, 0)
        store = ns if f == 0 else ds
        mine = pl.ds(pl.multiple_of(core * BLK, BLK), BLK)
        own = store[:, mine]
        other = sib[f]
        dims = (((0,), (0,)), ((), ()))
        for i in range(1, 5):
            q = (zc + i) % 4
            cut = pl.ds(pl.multiple_of(q * 256, 256), 256)
            own_cut = store[:, pl.ds(pl.multiple_of(core * BLK + q * 256, 256), 256)]
            part = lax.dot_general(own_cut, own, dims, preferred_element_type=F32)
            part = part + lax.dot_general(sib[f, :, cut], other, dims, preferred_element_type=F32)
            part = part.astype(BF16)
            for t in range(CHIPS):
                tile = part[:, t * SLAB : (t + 1) * SLAB]
                gram[f, t, cut, :] = tile
                if t < KEPT - 1:
                    gram[f, t + CHIPS, cut, :] = tile
            yp_copy(f, q).start()
            if i < 4:
                for y in range(2):
                    zq_copy(f, q, y).start()

    def mine_tile(f, k, t):
        return gram[f, k + t, pl.ds(pl.multiple_of(k * SLAB, SLAB), SLAB), :].astype(F32)

    def sum_gather(f):
        def relay(z):
            yp_copy(f, z).wait_recv()
            for t in range(YZ):
                ps[f, z, t] = (mine_tile(f, 2 * z + yc, t) + yp[f, z, t].astype(F32)).astype(BF16)
            zp_copy(f, z).start()

        other_z(relay)
        other_z(lambda z: zq_arrival(f, z, 1 - yc).wait_recv())
        for t in range(ZY):
            total = mine_tile(f, 2 * zc + 1 - yc, YZ + t)
            for i in range(1, 4):
                total = total + zq[f, (zc + i) % 4, 1 - yc, t].astype(F32)
            qs[f, t] = total.astype(BF16)
        yq_copy(f).start()
        yp_copy(f, zc).wait_recv()
        other_z(lambda z: zq_arrival(f, z, yc).wait_recv())
        other_z(lambda z: zp_arrival(f, z).wait_recv())
        ri = lax.broadcasted_iota(jnp.int32, (SLAB, SLAB), 0)
        ci = lax.broadcasted_iota(jnp.int32, (SLAB, SLAB), 1)
        eye = ri == ci

        def put(t, total):
            ag[f, chip, EXTRA + t * SLAB : EXTRA + (t + 1) * SLAB, :] = total.astype(BF16)

        for t in range(YZ):
            total = mine_tile(f, chip, t) + yp[f, zc, t].astype(F32)
            for i in range(1, 4):
                total = total + zp[f, (zc + i) % 4, t].astype(F32)
            total = total * (1.0 / ROW_TOTAL)
            if t == 0:
                diag = jnp.sum(jnp.where(eye, total, 0.0), axis=0, keepdims=True) + DAMPING
                high = diag.astype(BF16).astype(F32)
                row = lax.broadcasted_iota(jnp.int32, (EXTRA, SLAB), 0)
                extra = jnp.where(row == 0, high, jnp.where(row == 1, diag - high, 0.0))
                ag[f, chip, 0:EXTRA, :] = extra.astype(BF16)
                total = jnp.where(eye, 0.0, total)
            put(t, total)
        other_z(lambda z: gp_z(f, z).start())
        gp_y(f, zc).start()
        yq_copy(f).wait_recv()
        for t in range(ZY):
            total = mine_tile(f, chip, YZ + t) + yq[f, t].astype(F32)
            for i in range(1, 4):
                total = total + zq[f, (zc + i) % 4, yc, t].astype(F32)
            put(YZ + t, total * (1.0 / ROW_TOTAL))
        gq_y(f).start()
        other_z(lambda z: gq_z(f, z).start())

    def assemble(f, k):
        here = pl.ds(pl.multiple_of(k * SLAB, SLAB), SLAB)
        for j in range(KEPT):
            there = pl.ds(pl.multiple_of(((k + j) % CHIPS) * SLAB, SLAB), SLAB)
            tile = ag[f, k, EXTRA + j * SLAB : EXTRA + (j + 1) * SLAB, :]
            full[here, there] = tile
            if 0 < j < KEPT - 1:
                full[there, here] = tile.T
        dv[:, here] = jnp.sum(ag[f, k, 0:EXTRA, :].astype(F32), axis=0, keepdims=True)

    def gathered(f, k):
        gp_copy(f, k, gp_ysend.at[f, 0], ypeer).wait_recv()
        gq_copy(f, k, gq_ysend.at[f], ypeer).wait_recv()

    def roots(f, out):
        across = 2 * zc + 1 - yc

        def pass_on(z):
            gp_copy(f, 2 * z + yc, gp_ysend.at[f, z], ypeer).wait_recv()
            gp_y(f, z).start()

        pass_on((zc + 1) % 4)
        gathered(f, across)
        other_z(lambda z: gq_f(f, z).start())
        pass_on((zc + 3) % 4)
        pass_on((zc + 2) % 4)
        assemble(f, chip)
        assemble(f, across)

        def direct(z):
            gq_copy(f, 2 * z + yc, gq_ysend.at[f], ypeer).wait_recv()
            assemble(f, 2 * z + yc)

        def indirect(z):
            gathered(f, 2 * z + 1 - yc)
            assemble(f, 2 * z + 1 - yc)

        other_z(direct)
        other_z(indirect)
        diag = dv[...]
        ones = jnp.ones((16, BLK), BF16)
        bound = jnp.abs(diag) + jnp.dot(ones, jnp.abs(full[...]), preferred_element_type=F32)[:1]
        scale = 1.0 / jnp.max(bound, axis=1, keepdims=True)
        mine = pl.ds(pl.multiple_of(chip * SLAB, SLAB), SLAB)
        ri = lax.broadcasted_iota(jnp.int32, (SLAB, BLK), 0)
        ci = lax.broadcasted_iota(jnp.int32, (SLAB, BLK), 1)
        eye = ci == ri + chip * SLAB
        scaled_diag = diag * scale
        off = full[mine, :].astype(F32) * scale
        slab[0] = off
        slab[1] = jnp.where(eye, scaled_diag, off)

        def times(u):
            u_diag = jnp.sum(jnp.where(eye, u, 0.0), axis=1, keepdims=True)
            u_off = jnp.where(eye, 0.0, u).astype(BF16)
            prod = jnp.dot(u_off, full[...], preferred_element_type=F32) * scale
            return prod + u_diag * slab[0] + u * scaled_diag

        u = times(0.0625 * slab[1]) - 0.5625 * slab[1]
        u = times(u) + 1.6875 * slab[1]
        u = times(u) - 2.4375 * slab[1]
        ztile[f] = u + jnp.where(eye, 2.25, 0.0)
        cols = pl.ds(pl.multiple_of(core * BLK, BLK), BLK)
        to_sibling(f, out).start()
        to_out(f, out).start()

    def to_sibling(f, out):
        cols = pl.ds(pl.multiple_of(core * BLK, BLK), BLK)
        return pltpu.make_async_remote_copy(
            src_ref=ztile.at[f, pl.ds(pl.multiple_of((1 - core) * HALF, HALF), HALF), :], dst_ref=out.at[:, cols],
            send_sem=out_send.at[f], recv_sem=out_recv.at[f], device_id=sibling, device_id_type=MESH,
        )

    def to_out(f, out):
        cols = pl.ds(pl.multiple_of(core * BLK, BLK), BLK)
        return pltpu.make_async_copy(
            ztile.at[f, pl.ds(pl.multiple_of(core * HALF, HALF), HALF), :], out.at[:, cols], own_sem.at[f]
        )

    @pl.when(s >= 4)
    def _():
        transpose_weight()

    lag = jnp.minimum(M, (SECTIONS - 1 - s) * LAG)

    def first_half(i, _):
        forward_step(i)

        @pl.when(i >= lag)
        def _():
            backward_step(i - lag)

        return 0

    lax.fori_loop(0, M, first_half, 0)

    @pl.when((s >= 1) & (s < 4))
    def _():
        transpose_weight()

    @pl.when(s <= 4)
    def _():
        gram_send(0)

    @pl.when(s <= 3)
    def _():
        sum_gather(0)

    @pl.when(s <= 2)
    def _():
        roots(0, act_out)

    def second_half(i, _):
        backward_step(i)

        @pl.when((s == 4) & (i == 2))
        def _():
            sum_gather(0)

        return 0

    lax.fori_loop(M - lag, M, second_half, 0)

    @pl.when(s >= 5)
    def _():
        gram_send(0)

    gram_send(1)

    @pl.when(s >= 5)
    def _():
        sum_gather(0)

    sum_gather(1)

    @pl.when(s >= 3)
    def _():
        roots(0, act_out)

    roots(1, grad_out)

    for f, out in ((0, act_out), (1, grad_out)):
        to_out(f, out).wait()
        to_sibling(f, out).wait()

    def sent(m, _):
        @pl.when(s < SECTIONS - 1)
        def _():
            f_copy(m, whole).wait_send()

        @pl.when(s > 0)
        def _():
            b_copy(m, whole).wait_send()

        sib_copy(0, m).wait_send()
        sib_copy(1, m).wait_send()
        return 0

    lax.fori_loop(0, M, sent, 0)
    @pl.when(last)
    def _():
        cot_whole(0).wait_send()
        cot_whole(1).wait_send()

    for f in range(2):

        def z_sent(z):
            zq_copy(f, z, 0).wait_send()
            zq_copy(f, z, 1).wait_send()
            zp_copy(f, z).wait_send()
            gp_z(f, z).wait_send()
            gp_y(f, z).wait_send()
            yp_copy(f, z).wait_send()
            gq_z(f, z).wait_send()
            gq_f(f, z).wait_send()

        other_z(z_sent)
        yp_copy(f, zc).wait_send()
        gp_y(f, zc).wait_send()
        yq_copy(f).wait_send()
        gq_y(f).wait_send()


def copy_kernel(act, grad, act_out, grad_out, held, sems):
    loads = [pltpu.make_async_copy(act, held.at[0], sems.at[0]), pltpu.make_async_copy(grad, held.at[1], sems.at[1])]
    stores = [pltpu.make_async_copy(held.at[0], act_out, sems.at[2]), pltpu.make_async_copy(held.at[1], grad_out, sems.at[3])]
    for cp in loads:
        cp.start()
    for load, store in zip(loads, stores):
        load.wait()
        store.start()
    for cp in stores:
        cp.wait()


def shards(tokens, cotangent, gain, weight):
    out = jax.ShapeDtypeStruct((HALF, D), F32)
    dma = pltpu.SemaphoreType.DMA
    anywhere = pl.BlockSpec(memory_space=pl.ANY)
    chunks = (M, R, D)
    act, grad = pl.pallas_call(
        kernel,
        out_shape=(out, out),
        in_specs=[anywhere, anywhere, pl.BlockSpec(memory_space=pltpu.VMEM), anywhere],
        out_specs=(anywhere, anywhere),
        scratch_shapes=[
            pltpu.VMEM((D, D), BF16),
            pltpu.VMEM((D, D), BF16),
            pltpu.VMEM((M, NT, R, TN), BF16),
            pltpu.VMEM((M, NT, R, TN), BF16),
            pltpu.VMEM((M, NT, R, TN), BF16),
            pltpu.VMEM((M, NT, R, TN), BF16),
            pltpu.VMEM((ROWS, D), F32),
            pltpu.VMEM((ROWS, D), F32),
            pltpu.VMEM((ROWS, D), BF16),
            pltpu.VMEM((ROWS, D), BF16),
            pltpu.VMEM((ROWS, 128), F32),
            pltpu.VMEM((2, ROWS, BLK), BF16),
            pltpu.VMEM((2, CHIPS + KEPT - 1, BLK, SLAB), BF16),
            pltpu.VMEM((2, 4, YZ, SLAB, SLAB), BF16),
            pltpu.VMEM((2, 4, 2, ZY, SLAB, SLAB), BF16),
            pltpu.VMEM((2, 4, YZ, SLAB, SLAB), BF16),
            pltpu.VMEM((2, ZY, SLAB, SLAB), BF16),
            pltpu.VMEM((2, 4, YZ, SLAB, SLAB), BF16),
            pltpu.VMEM((2, ZY, SLAB, SLAB), BF16),
            pltpu.VMEM((2, CHIPS, EXTRA + KEPT * SLAB, SLAB), BF16),
            pltpu.VMEM((BLK, BLK), BF16),
            pltpu.VMEM((1, BLK), F32),
            pltpu.VMEM((2, SLAB, BLK), F32),
            pltpu.VMEM((2, SLAB, BLK), F32),
            pltpu.VMEM((2, PAD, D), BF16),
            dma((NT,)),
            dma((2,)),
            dma((M,)),
            dma((M,)),
            dma((M,)),
            dma((M,)),
            dma((2, M)),
            dma((2, M)),
            dma((2, 4)),
            dma((2, 4)),
            dma((2, 4, 2)),
            dma((2, 4, 2)),
            dma((2, 4)),
            dma((2, 4)),
            dma((2,)),
            dma((2,)),
            dma((2, 4)),
            dma((2, 4)),
            dma((2, CHIPS)),
            dma((2,)),
            dma((2, 4)),
            dma((2, 4)),
            dma((2, CHIPS)),
            dma((2,)),
            dma((2,)),
            dma((2,)),
            dma((2,)),
        ],
        name="refresh",
        compiler_params=pltpu.CompilerParams(
            collective_id=0, has_side_effects=True, vmem_limit_bytes=58 * 2**20
        ),
    )(tokens.reshape(chunks), cotangent.reshape(chunks), gain, weight)
    return pl.pallas_call(
        copy_kernel,
        out_shape=(out, out),
        in_specs=[anywhere] * 2,
        out_specs=(anywhere, anywhere),
        scratch_shapes=[pltpu.VMEM((2, HALF, D), F32), dma((4,))],
        name="results",
    )(act, grad)


def solution(mesh):
    return jax.shard_map(
        shards,
        mesh=mesh,
        in_specs=(P(None, "dp", None), P(None, "dp", None), P("section", None), P("section", None)),
        out_specs=(P(("section", "dp"), None), P(("section", "dp"), None)),
        check_vma=False,
    )
```

```python
import functools

import jax
import jax.numpy as jnp
from jax import lax
from jax.experimental import pallas as pl
from jax.experimental.pallas import tpu as pltpu
from jax.sharding import PartitionSpec as P

MESH = pl.DeviceIdType.MESH
F32 = jnp.float32
BF16 = jnp.bfloat16

D = 2048
BLK = 1024
ROWS = 256
R = 32
M = ROWS // R
TN = 256
NT = D // TN
CHIPS = 8
SLAB = BLK // CHIPS
HALF = SLAB // 2
KEPT = 5
YZ = 2
ZY = KEPT - YZ
EXTRA = 16
SPLIT = EXTRA + YZ * SLAB
ROW_TOTAL = 4096.0
DAMPING = 4.0
SECTIONS = 8
LAG = 3
PAD = 128
GROUPS = ((0, 4, 2), (4, 8, 2))

GELU_A = 0.7978845608028654
GELU_B = 0.044715


def gelu_value(z):
    t = jnp.tanh(GELU_A * (z + GELU_B * (z * z * z)))
    return 0.5 * z * (1.0 + t)


def gelu_slope(z):
    sq = z * z
    t = jnp.tanh(GELU_A * (z + GELU_B * (sq * z)))
    return 0.5 * (1.0 + t) + 0.5 * z * (1.0 - t * t) * (GELU_A * (1.0 + 3.0 * GELU_B * sq))


def kernel(
    tok, cot, gain, wgt, act_out, grad_out,
    w, wt, xs, ys, sendf, sendb, zs, slopes, ns, ds, rinvs, sib, gram, zp, ag, full, dv, slab, ztile, lhs,
    w_sem, tok_sem, f_send, f_recv, b_send, b_recv, sib_send, sib_recv,
    zp_send, zp_recv,
    gp_zsend, gp_ysend, gp_recv, gq_ysend, gq_zsend, gq_fsend, gq_recv, cot_send, own_sem, out_send, out_recv,
):
    s = lax.axis_index("section")
    d = lax.axis_index("dp")
    chip = d // 2
    core = d % 2
    zc = d // 4
    yc = (d // 2) % 2
    flipped = zc * 4 + (1 - yc) * 2 + core
    nxt = (jnp.minimum(s + 1, SECTIONS - 1), jnp.where(s == 3, flipped, d))
    prv = (jnp.maximum(s - 1, 0), jnp.where(s == 4, flipped, d))
    ypeer = (s, flipped)
    ydiag = (s, zc * 4 + (1 - yc) * 2 + 1 - core)
    sibling = (s, chip * 2 + 1 - core)
    first = s == 0
    last = s == SECTIONS - 1

    def zpeer(z):
        return (s, z * 4 + yc * 2 + core)

    def remote(src, dst, send_sem, recv_sem, device):
        return pltpu.make_async_remote_copy(
            src_ref=src, dst_ref=dst, send_sem=send_sem, recv_sem=recv_sem, device_id=device, device_id_type=MESH
        )

    def w_copy(j):
        cols = pl.ds(j * TN, TN)
        return pltpu.make_async_copy(wgt.at[:, cols], w.at[:, cols], w_sem.at[j])

    def first_load(source, target, j):
        cols = pl.ds(j * TN, TN)
        return pltpu.make_async_copy(source.at[0, :, cols], target.at[0, j], tok_sem.at[0])

    def cot_copy(part, j):
        cols = pl.ds(j * TN, TN)
        chunk = 0 if part == 0 else slice(1, M)
        return remote(cot.at[chunk, :, cols], ys.at[chunk, j], cot_send.at[part], tok_sem.at[part], ypeer)

    def cot_whole(part):
        chunk = ys.at[0] if part == 0 else ys.at[1:M]
        return remote(chunk, chunk, cot_send.at[part], tok_sem.at[part], ypeer)

    def rest_load(source, target, j):
        cols = pl.ds(j * TN, TN)
        return pltpu.make_async_copy(source.at[1:M, :, cols], target.at[1:M, j], tok_sem.at[1])

    def loaded(target, m):
        @pl.when(m == 0)
        def _():
            pltpu.make_async_copy(target.at[0], target.at[0], tok_sem.at[0]).wait()

        @pl.when(m == 1)
        def _():
            pltpu.make_async_copy(target.at[1:M], target.at[1:M], tok_sem.at[1]).wait()

    @pl.when(first)
    def _():
        for j in range(NT):
            first_load(tok, xs, j).start()

    for j in range(NT):
        w_copy(j).start()

    @pl.when(first)
    def _():
        for j in range(NT):
            rest_load(tok, xs, j).start()

    lhs[...] = jnp.zeros_like(lhs)

    barrier = pltpu.get_barrier_semaphore()
    for neighbour in [sibling, ypeer, ydiag] + [zpeer((zc + i) % 4) for i in range(1, 4)]:
        pl.semaphore_signal(barrier, inc=1, device_id=neighbour, device_id_type=MESH)

    @pl.when(s < SECTIONS - 1)
    def _():
        pl.semaphore_signal(barrier, inc=1, device_id=nxt, device_id_type=MESH)

    @pl.when(s > 0)
    def _():
        pl.semaphore_signal(barrier, inc=1, device_id=prv, device_id_type=MESH)

    pl.semaphore_wait(barrier, 6 + jnp.where(first, 0, 1) + jnp.where(last, 0, 1))

    @pl.when(last)
    def _():
        for j in range(NT):
            cot_copy(0, j).start()
        for j in range(NT):
            cot_copy(1, j).start()

    @pl.when(s > 0)
    def _():
        for j in range(NT):
            w_copy(j).wait()

    def transpose_weight():
        def body(k, _):
            kr = pl.ds(pl.multiple_of(k * TN, TN), TN)
            for j in range(NT):
                wt[j * TN : (j + 1) * TN, kr] = w[kr, j * TN : (j + 1) * TN].T
            return 0

        lax.fori_loop(0, NT, body, 0)

    def chunk_rows(m):
        return pl.ds(pl.multiple_of(m * R, R), R)

    def f_copy(m, part):
        return pltpu.make_async_remote_copy(
            src_ref=sendf.at[m, part], dst_ref=xs.at[m, part],
            send_sem=f_send.at[m], recv_sem=f_recv.at[m], device_id=nxt, device_id_type=MESH,
        )

    def b_copy(m, part):
        return pltpu.make_async_remote_copy(
            src_ref=sendb.at[m, part], dst_ref=ys.at[m, part],
            send_sem=b_send.at[m], recv_sem=b_recv.at[m], device_id=prv, device_id_type=MESH,
        )

    whole = pl.ds(0, NT)

    near = (sibling, ypeer, ydiag)

    def sib_copy(f, m, p):
        rows = chunk_rows(m)
        store = ns if f == 0 else ds
        block = core if p == 1 else 1 - core
        return remote(
            store.at[rows, pl.ds(pl.multiple_of(block * BLK, BLK), BLK)], sib.at[f, p, rows, :],
            sib_send.at[f, p, m], sib_recv.at[f, p, m], near[p],
        )

    def share(f, m):
        for p in range(3):
            sib_copy(f, m, p).start()

    def forward(m, send, fresh=False):
        rows = chunk_rows(m)
        total = jnp.zeros((R, TN), F32)
        for j in range(NT):
            xj = xs[m, j].astype(F32)
            total = total + xj * xj
        rinv = lax.rsqrt(jnp.sum(total, axis=-1, keepdims=True) * (1.0 / D) + 1e-06)
        rinvs[rows, :] = jnp.broadcast_to(rinv, (R, 128))
        for j in range(NT):
            cols = slice(j * TN, (j + 1) * TN)
            normed = (xs[m, j].astype(F32) * rinv * gain[:, cols]).astype(BF16)
            ns[rows, cols] = normed
            lhs[0, :R, cols] = normed
        padded = lhs[0]
        for j in range(NT):
            cols = slice(j * TN, (j + 1) * TN)
            if fresh:
                w_copy(j).wait()
            z = jnp.dot(padded, w[:, cols], preferred_element_type=F32)[:R]
            zs[rows, cols] = z
            if send:
                sendf[m, j] = (xs[m, j].astype(F32) + gelu_value(z)).astype(BF16)
                for lo, hi, step in GROUPS:
                    if j + 1 == hi:
                        for part in range(lo, hi, step):
                            f_copy(m, pl.ds(part, step)).start()
        share(0, m)
        for j in range(NT):
            cols = slice(j * TN, (j + 1) * TN)
            slopes[rows, cols] = gelu_slope(zs[rows, cols])

    def backward(m, send):
        rows = chunk_rows(m)
        total = jnp.zeros((R, TN), F32)
        for j in range(NT):
            cols = slice(j * TN, (j + 1) * TN)
            z = zs[rows, cols]
            delta = (ys[m, j].astype(F32) * slopes[rows, cols]).astype(BF16)
            ds[rows, cols] = delta
            lhs[1, :R, cols] = delta
            total = total + delta.astype(F32) * z
        if send:
            rinv = rinvs[rows, :1]
            pull = jnp.sum(total, axis=-1, keepdims=True) * (1.0 / D) * rinv
            padded = lhs[1]
            for j in range(NT):
                cols = slice(j * TN, (j + 1) * TN)
                dn = jnp.dot(padded, wt[:, cols], preferred_element_type=F32)[:R]
                xj = xs[m, j].astype(F32)
                dy = ys[m, j].astype(F32) + rinv * (dn * gain[:, cols] - xj * pull)
                sendb[m, j] = dy.astype(BF16)
                for lo, hi, step in GROUPS:
                    if j + 1 == hi:
                        for part in range(lo, hi, step):
                            b_copy(m, pl.ds(part, step)).start()
        share(1, m)

    def forward_step(m):
        @pl.when(s > 0)
        def _():
            f_copy(m, whole).wait_recv()

        @pl.when(first)
        def _():
            loaded(xs, m)

        @pl.when(first & (m == 0))
        def _():
            forward(m, True, True)

        @pl.when((s < SECTIONS - 1) & ((s > 0) | (m > 0)))
        def _():
            forward(m, True)

        @pl.when(last)
        def _():
            forward(m, False)

    def backward_step(m):
        @pl.when(s < SECTIONS - 1)
        def _():
            b_copy(m, whole).wait_recv()

        @pl.when(last & (m == 0))
        def _():
            cot_whole(0).wait_recv()

        @pl.when(last & (m == 1))
        def _():
            cot_whole(1).wait_recv()

        @pl.when(s > 0)
        def _():
            backward(m, True)

        @pl.when(first)
        def _():
            backward(m, False)

    def slab_of(f, k, tile, count):
        return gram.at[f, pl.ds(k + tile, count), pl.ds(pl.multiple_of(k * SLAB, SLAB), SLAB), :]

    def zp_copy(f, z):
        src = slab_of(f, 2 * z + yc, 0, KEPT)
        return remote(src, zp.at[f, zc], zp_send.at[f, z], zp_recv.at[f, zc], zpeer(z))

    def zp_arrival(f, z):
        return remote(zp.at[f, z], zp.at[f, z], zp_send.at[f, z], zp_recv.at[f, z], zpeer(z))

    def gp_copy(f, k, send_sem, device):
        part = ag.at[f, k, pl.ds(0, SPLIT), :]
        return remote(part, part, send_sem, gp_recv.at[f, k], device)

    def gq_copy(f, k, send_sem, device):
        part = ag.at[f, k, pl.ds(SPLIT, ZY * SLAB), :]
        return remote(part, part, send_sem, gq_recv.at[f, k], device)

    def gp_z(f, z):
        return gp_copy(f, chip, gp_zsend.at[f, z], zpeer(z))

    def gp_y(f, z):
        return gp_copy(f, 2 * z + yc, gp_ysend.at[f, z], ypeer)

    def gq_y(f):
        return gq_copy(f, chip, gq_ysend.at[f], ypeer)

    def gq_z(f, z):
        return gq_copy(f, chip, gq_zsend.at[f, z], zpeer(z))

    def gq_f(f, z):
        return gq_copy(f, 2 * zc + 1 - yc, gq_fsend.at[f, z], zpeer(z))

    def other_z(fn):
        def body(i, _):
            fn((zc + i) % 4)
            return 0

        lax.fori_loop(1, 4, body, 0)

    def gram_send(f):
        def landed(m, _):
            for p in range(3):
                sib_copy(f, m, p).wait_recv()
            return 0

        lax.fori_loop(0, M, landed, 0)
        store = ns if f == 0 else ds
        own = store[:, pl.ds(pl.multiple_of(core * BLK, BLK), BLK)]
        dims = (((0,), (0,)), ((), ()))
        for i in range(1, 5):
            q = (zc + i) % 4
            k = 2 * q + yc
            cut = pl.ds(pl.multiple_of(k * SLAB, SLAB), SLAB)
            own_cut = store[:, pl.ds(pl.multiple_of(core * BLK + k * SLAB, SLAB), SLAB)]
            part = lax.dot_general(own_cut, own, dims, preferred_element_type=F32)
            for p in range(3):
                part = part + lax.dot_general(sib[f, p, :, cut], sib[f, p], dims, preferred_element_type=F32)
            part = part.astype(BF16)
            for t in range(CHIPS):
                tile = part[:, t * SLAB : (t + 1) * SLAB]
                gram[f, t, cut, :] = tile
                if t < KEPT - 1:
                    gram[f, t + CHIPS, cut, :] = tile
            if i < 4:
                zp_copy(f, q).start()

    def mine_tile(f, k, t):
        return gram[f, k + t, pl.ds(pl.multiple_of(k * SLAB, SLAB), SLAB), :].astype(F32)

    def sum_gather(f):
        other_z(lambda z: zp_arrival(f, z).wait_recv())
        ri = lax.broadcasted_iota(jnp.int32, (SLAB, SLAB), 0)
        ci = lax.broadcasted_iota(jnp.int32, (SLAB, SLAB), 1)
        eye = ri == ci

        def put(t, total):
            ag[f, chip, EXTRA + t * SLAB : EXTRA + (t + 1) * SLAB, :] = total.astype(BF16)

        for t in range(KEPT):
            total = mine_tile(f, chip, t)
            for i in range(1, 4):
                total = total + zp[f, (zc + i) % 4, t].astype(F32)
            total = total * (1.0 / ROW_TOTAL)
            if t == 0:
                diag = jnp.sum(jnp.where(eye, total, 0.0), axis=0, keepdims=True) + DAMPING
                high = diag.astype(BF16).astype(F32)
                row = lax.broadcasted_iota(jnp.int32, (EXTRA, SLAB), 0)
                extra = jnp.where(row == 0, high, jnp.where(row == 1, diag - high, 0.0))
                ag[f, chip, 0:EXTRA, :] = extra.astype(BF16)
                total = jnp.where(eye, 0.0, total)
            ag[f, chip, EXTRA + t * SLAB : EXTRA + (t + 1) * SLAB, :] = total.astype(BF16)
            if t == YZ - 1:
                other_z(lambda z: gp_z(f, z).start())
                gp_y(f, zc).start()
        gq_y(f).start()
        other_z(lambda z: gq_z(f, z).start())

    def assemble(f, k):
        here = pl.ds(pl.multiple_of(k * SLAB, SLAB), SLAB)
        for j in range(KEPT):
            there = pl.ds(pl.multiple_of(((k + j) % CHIPS) * SLAB, SLAB), SLAB)
            tile = ag[f, k, EXTRA + j * SLAB : EXTRA + (j + 1) * SLAB, :]
            full[here, there] = tile
            if 0 < j < KEPT - 1:
                full[there, here] = tile.T
        dv[:, here] = jnp.sum(ag[f, k, 0:EXTRA, :].astype(F32), axis=0, keepdims=True)

    def gathered(f, k):
        gp_copy(f, k, gp_ysend.at[f, 0], ypeer).wait_recv()
        gq_copy(f, k, gq_ysend.at[f], ypeer).wait_recv()

    def roots(f, out):
        across = 2 * zc + 1 - yc

        def pass_on(z):
            gp_copy(f, 2 * z + yc, gp_ysend.at[f, z], ypeer).wait_recv()
            gp_y(f, z).start()

        pass_on((zc + 1) % 4)
        gathered(f, across)
        other_z(lambda z: gq_f(f, z).start())
        pass_on((zc + 3) % 4)
        pass_on((zc + 2) % 4)
        assemble(f, chip)
        assemble(f, across)

        def direct(z):
            gq_copy(f, 2 * z + yc, gq_ysend.at[f], ypeer).wait_recv()
            assemble(f, 2 * z + yc)

        def indirect(z):
            gathered(f, 2 * z + 1 - yc)
            assemble(f, 2 * z + 1 - yc)

        other_z(direct)
        other_z(indirect)
        diag = dv[...]
        ones = jnp.ones((16, BLK), BF16)
        bound = jnp.abs(diag) + jnp.dot(ones, jnp.abs(full[...]), preferred_element_type=F32)[:1]
        scale = 1.0 / jnp.max(bound, axis=1, keepdims=True)
        mine = pl.ds(pl.multiple_of(chip * SLAB, SLAB), SLAB)
        ri = lax.broadcasted_iota(jnp.int32, (SLAB, BLK), 0)
        ci = lax.broadcasted_iota(jnp.int32, (SLAB, BLK), 1)
        eye = ci == ri + chip * SLAB
        scaled_diag = diag * scale
        off = full[mine, :].astype(F32) * scale
        slab[0] = off
        slab[1] = jnp.where(eye, scaled_diag, off)

        def times(u):
            u_diag = jnp.sum(jnp.where(eye, u, 0.0), axis=1, keepdims=True)
            u_off = jnp.where(eye, 0.0, u).astype(BF16)
            prod = jnp.dot(u_off, full[...], preferred_element_type=F32) * scale
            return prod + u_diag * slab[0] + u * scaled_diag

        u = times(0.0625 * slab[1]) - 0.5625 * slab[1]
        u = times(u) + 1.6875 * slab[1]
        u = times(u) - 2.4375 * slab[1]
        ztile[f] = u + jnp.where(eye, 2.25, 0.0)
        cols = pl.ds(pl.multiple_of(core * BLK, BLK), BLK)
        to_sibling(f, out).start()
        to_out(f, out).start()

    def to_sibling(f, out):
        cols = pl.ds(pl.multiple_of(core * BLK, BLK), BLK)
        return pltpu.make_async_remote_copy(
            src_ref=ztile.at[f, pl.ds(pl.multiple_of((1 - core) * HALF, HALF), HALF), :], dst_ref=out.at[:, cols],
            send_sem=out_send.at[f], recv_sem=out_recv.at[f], device_id=sibling, device_id_type=MESH,
        )

    def to_out(f, out):
        cols = pl.ds(pl.multiple_of(core * BLK, BLK), BLK)
        return pltpu.make_async_copy(
            ztile.at[f, pl.ds(pl.multiple_of(core * HALF, HALF), HALF), :], out.at[:, cols], own_sem.at[f]
        )

    @pl.when(s >= 4)
    def _():
        transpose_weight()

    lag = jnp.minimum(M, (SECTIONS - 1 - s) * LAG)

    def first_half(i, _):
        forward_step(i)

        @pl.when(i >= lag)
        def _():
            backward_step(i - lag)

        return 0

    lax.fori_loop(0, M, first_half, 0)

    @pl.when((s >= 1) & (s < 4))
    def _():
        transpose_weight()

    @pl.when(s <= 4)
    def _():
        gram_send(0)

    @pl.when(s <= 3)
    def _():
        sum_gather(0)

    @pl.when(s <= 2)
    def _():
        roots(0, act_out)

    def second_half(i, _):
        backward_step(i)

        @pl.when((s == 4) & (i == 2))
        def _():
            sum_gather(0)

        return 0

    lax.fori_loop(M - lag, M, second_half, 0)

    @pl.when(s >= 5)
    def _():
        gram_send(0)

    gram_send(1)

    @pl.when(s >= 5)
    def _():
        sum_gather(0)

    sum_gather(1)

    @pl.when(s >= 3)
    def _():
        roots(0, act_out)

    roots(1, grad_out)

    for f, out in ((0, act_out), (1, grad_out)):
        to_out(f, out).wait()
        to_sibling(f, out).wait()

    def sent(m, _):
        @pl.when(s < SECTIONS - 1)
        def _():
            f_copy(m, whole).wait_send()

        @pl.when(s > 0)
        def _():
            b_copy(m, whole).wait_send()

        for p in range(3):
            sib_copy(0, m, p).wait_send()
            sib_copy(1, m, p).wait_send()
        return 0

    lax.fori_loop(0, M, sent, 0)
    @pl.when(last)
    def _():
        cot_whole(0).wait_send()
        cot_whole(1).wait_send()

    for f in range(2):

        def z_sent(z):
            zp_copy(f, z).wait_send()
            gp_z(f, z).wait_send()
            gp_y(f, z).wait_send()
            gq_z(f, z).wait_send()
            gq_f(f, z).wait_send()

        other_z(z_sent)
        gp_y(f, zc).wait_send()
        gq_y(f).wait_send()


def copy_kernel(act, grad, act_out, grad_out, held, sems):
    loads = [pltpu.make_async_copy(act, held.at[0], sems.at[0]), pltpu.make_async_copy(grad, held.at[1], sems.at[1])]
    stores = [pltpu.make_async_copy(held.at[0], act_out, sems.at[2]), pltpu.make_async_copy(held.at[1], grad_out, sems.at[3])]
    for cp in loads:
        cp.start()
    for load, store in zip(loads, stores):
        load.wait()
        store.start()
    for cp in stores:
        cp.wait()


def shards(tokens, cotangent, gain, weight):
    out = jax.ShapeDtypeStruct((HALF, D), F32)
    dma = pltpu.SemaphoreType.DMA
    anywhere = pl.BlockSpec(memory_space=pl.ANY)
    chunks = (M, R, D)
    act, grad = pl.pallas_call(
        kernel,
        out_shape=(out, out),
        in_specs=[anywhere, anywhere, pl.BlockSpec(memory_space=pltpu.VMEM), anywhere],
        out_specs=(anywhere, anywhere),
        scratch_shapes=[
            pltpu.VMEM((D, D), BF16),
            pltpu.VMEM((D, D), BF16),
            pltpu.VMEM((M, NT, R, TN), BF16),
            pltpu.VMEM((M, NT, R, TN), BF16),
            pltpu.VMEM((M, NT, R, TN), BF16),
            pltpu.VMEM((M, NT, R, TN), BF16),
            pltpu.VMEM((ROWS, D), F32),
            pltpu.VMEM((ROWS, D), F32),
            pltpu.VMEM((ROWS, D), BF16),
            pltpu.VMEM((ROWS, D), BF16),
            pltpu.VMEM((ROWS, 128), F32),
            pltpu.VMEM((2, 3, ROWS, BLK), BF16),
            pltpu.VMEM((2, CHIPS + KEPT - 1, BLK, SLAB), BF16),
            pltpu.VMEM((2, 4, KEPT, SLAB, SLAB), BF16),
            pltpu.VMEM((2, CHIPS, EXTRA + KEPT * SLAB, SLAB), BF16),
            pltpu.VMEM((BLK, BLK), BF16),
            pltpu.VMEM((1, BLK), F32),
            pltpu.VMEM((2, SLAB, BLK), F32),
            pltpu.VMEM((2, SLAB, BLK), F32),
            pltpu.VMEM((2, PAD, D), BF16),
            dma((NT,)),
            dma((2,)),
            dma((M,)),
            dma((M,)),
            dma((M,)),
            dma((M,)),
            dma((2, 3, M)),
            dma((2, 3, M)),
            dma((2, 4)),
            dma((2, 4)),
            dma((2, 4)),
            dma((2, 4)),
            dma((2, CHIPS)),
            dma((2,)),
            dma((2, 4)),
            dma((2, 4)),
            dma((2, CHIPS)),
            dma((2,)),
            dma((2,)),
            dma((2,)),
            dma((2,)),
        ],
        name="refresh",
        compiler_params=pltpu.CompilerParams(
            collective_id=0, has_side_effects=True, vmem_limit_bytes=58 * 2**20
        ),
    )(tokens.reshape(chunks), cotangent.reshape(chunks), gain, weight)
    return pl.pallas_call(
        copy_kernel,
        out_shape=(out, out),
        in_specs=[anywhere] * 2,
        out_specs=(anywhere, anywhere),
        scratch_shapes=[pltpu.VMEM((2, HALF, D), F32), dma((4,))],
        name="results",
    )(act, grad)


def solution(mesh):
    return jax.shard_map(
        shards,
        mesh=mesh,
        in_specs=(P(None, "dp", None), P(None, "dp", None), P("section", None), P("section", None)),
        out_specs=(P(("section", "dp"), None), P(("section", "dp"), None)),
        check_vma=False,
    )
```

```python
import functools

import jax
import jax.numpy as jnp
from jax import lax
from jax.experimental import pallas as pl
from jax.experimental.pallas import tpu as pltpu
from jax.sharding import PartitionSpec as P

MESH = pl.DeviceIdType.MESH
F32 = jnp.float32
BF16 = jnp.bfloat16

D = 2048
BLK = 1024
ROWS = 256
R = 32
M = ROWS // R
TN = 256
NT = D // TN
CHIPS = 8
SLAB = BLK // CHIPS
HALF = SLAB // 2
KEPT = 5
YZ = 2
ZY = KEPT - YZ
EXTRA = 16
SPLIT = EXTRA + YZ * SLAB
ROW_TOTAL = 4096.0
DAMPING = 4.0
SECTIONS = 8
LAG = 3
PAD = 128
GROUPS = ((0, 4, 2), (4, 8, 2))

GELU_A = 0.7978845608028654
GELU_B = 0.044715


def gelu_value(z):
    t = jnp.tanh(GELU_A * (z + GELU_B * (z * z * z)))
    return 0.5 * z * (1.0 + t)


def gelu_slope(z):
    sq = z * z
    t = jnp.tanh(GELU_A * (z + GELU_B * (sq * z)))
    return 0.5 * (1.0 + t) + 0.5 * z * (1.0 - t * t) * (GELU_A * (1.0 + 3.0 * GELU_B * sq))


def kernel(
    tok, cot, gain, wgt, act_out, grad_out,
    w, wt, xs, ys, sendf, sendb, zs, slopes, ns, ds, rinvs, sib, partial, gram, zp, ag, full, dv, slab, ztile, lhs,
    w_sem, tok_sem, f_send, f_recv, b_send, b_recv, sib_send, sib_recv,
    zp_send, zp_recv,
    gp_zsend, gp_ysend, gp_recv, gq_ysend, gq_zsend, gq_fsend, gq_recv, cot_send, own_sem, out_send, out_recv,
):
    s = lax.axis_index("section")
    d = lax.axis_index("dp")
    chip = d // 2
    core = d % 2
    zc = d // 4
    yc = (d // 2) % 2
    flipped = zc * 4 + (1 - yc) * 2 + core
    nxt = (jnp.minimum(s + 1, SECTIONS - 1), jnp.where(s == 3, flipped, d))
    prv = (jnp.maximum(s - 1, 0), jnp.where(s == 4, flipped, d))
    ypeer = (s, flipped)
    ydiag = (s, zc * 4 + (1 - yc) * 2 + 1 - core)
    sibling = (s, chip * 2 + 1 - core)
    first = s == 0
    last = s == SECTIONS - 1

    def zpeer(z):
        return (s, z * 4 + yc * 2 + core)

    def remote(src, dst, send_sem, recv_sem, device):
        return pltpu.make_async_remote_copy(
            src_ref=src, dst_ref=dst, send_sem=send_sem, recv_sem=recv_sem, device_id=device, device_id_type=MESH
        )

    def w_copy(j):
        cols = pl.ds(j * TN, TN)
        return pltpu.make_async_copy(wgt.at[:, cols], w.at[:, cols], w_sem.at[j])

    def first_load(source, target, j):
        cols = pl.ds(j * TN, TN)
        return pltpu.make_async_copy(source.at[0, :, cols], target.at[0, j], tok_sem.at[0])

    def cot_copy(part, j):
        cols = pl.ds(j * TN, TN)
        chunk = 0 if part == 0 else slice(1, M)
        return remote(cot.at[chunk, :, cols], ys.at[chunk, j], cot_send.at[part], tok_sem.at[part], ypeer)

    def cot_whole(part):
        chunk = ys.at[0] if part == 0 else ys.at[1:M]
        return remote(chunk, chunk, cot_send.at[part], tok_sem.at[part], ypeer)

    def rest_load(source, target, j):
        cols = pl.ds(j * TN, TN)
        return pltpu.make_async_copy(source.at[1:M, :, cols], target.at[1:M, j], tok_sem.at[1])

    def loaded(target, m):
        @pl.when(m == 0)
        def _():
            pltpu.make_async_copy(target.at[0], target.at[0], tok_sem.at[0]).wait()

        @pl.when(m == 1)
        def _():
            pltpu.make_async_copy(target.at[1:M], target.at[1:M], tok_sem.at[1]).wait()

    @pl.when(first)
    def _():
        for j in range(NT):
            first_load(tok, xs, j).start()

    for j in range(NT):
        w_copy(j).start()

    @pl.when(first)
    def _():
        for j in range(NT):
            rest_load(tok, xs, j).start()

    lhs[...] = jnp.zeros_like(lhs)

    barrier = pltpu.get_barrier_semaphore()
    for neighbour in [sibling, ypeer, ydiag] + [zpeer((zc + i) % 4) for i in range(1, 4)]:
        pl.semaphore_signal(barrier, inc=1, device_id=neighbour, device_id_type=MESH)

    @pl.when(s < SECTIONS - 1)
    def _():
        pl.semaphore_signal(barrier, inc=1, device_id=nxt, device_id_type=MESH)

    @pl.when(s > 0)
    def _():
        pl.semaphore_signal(barrier, inc=1, device_id=prv, device_id_type=MESH)

    pl.semaphore_wait(barrier, 6 + jnp.where(first, 0, 1) + jnp.where(last, 0, 1))

    @pl.when(last)
    def _():
        for j in range(NT):
            cot_copy(0, j).start()
        for j in range(NT):
            cot_copy(1, j).start()

    @pl.when(s > 0)
    def _():
        for j in range(NT):
            w_copy(j).wait()

    def transpose_weight():
        def body(k, _):
            kr = pl.ds(pl.multiple_of(k * TN, TN), TN)
            for j in range(NT):
                wt[j * TN : (j + 1) * TN, kr] = w[kr, j * TN : (j + 1) * TN].T
            return 0

        lax.fori_loop(0, NT, body, 0)

    def chunk_rows(m):
        return pl.ds(pl.multiple_of(m * R, R), R)

    def f_copy(m, part):
        return pltpu.make_async_remote_copy(
            src_ref=sendf.at[m, part], dst_ref=xs.at[m, part],
            send_sem=f_send.at[m], recv_sem=f_recv.at[m], device_id=nxt, device_id_type=MESH,
        )

    def b_copy(m, part):
        return pltpu.make_async_remote_copy(
            src_ref=sendb.at[m, part], dst_ref=ys.at[m, part],
            send_sem=b_send.at[m], recv_sem=b_recv.at[m], device_id=prv, device_id_type=MESH,
        )

    whole = pl.ds(0, NT)

    near = (sibling, ypeer, ydiag)

    def sib_copy(f, m, p):
        rows = chunk_rows(m)
        store = ns if f == 0 else ds
        block = core if p == 1 else 1 - core
        return remote(
            store.at[rows, pl.ds(pl.multiple_of(block * BLK, BLK), BLK)], sib.at[f, p, rows, :],
            sib_send.at[f, p, m], sib_recv.at[f, p, m], near[p],
        )

    def share(f, m):
        for p in (1, 2, 0):
            sib_copy(f, m, p).start()

    def forward(m, send, fresh=False):
        rows = chunk_rows(m)
        total = jnp.zeros((R, TN), F32)
        for j in range(NT):
            xj = xs[m, j].astype(F32)
            total = total + xj * xj
        rinv = lax.rsqrt(jnp.sum(total, axis=-1, keepdims=True) * (1.0 / D) + 1e-06)
        rinvs[rows, :] = jnp.broadcast_to(rinv, (R, 128))
        for j in range(NT):
            cols = slice(j * TN, (j + 1) * TN)
            normed = (xs[m, j].astype(F32) * rinv * gain[:, cols]).astype(BF16)
            ns[rows, cols] = normed
            lhs[0, :R, cols] = normed
        padded = lhs[0]
        for j in range(NT):
            cols = slice(j * TN, (j + 1) * TN)
            if fresh:
                w_copy(j).wait()
            z = jnp.dot(padded, w[:, cols], preferred_element_type=F32)[:R]
            zs[rows, cols] = z
            if send:
                sendf[m, j] = (xs[m, j].astype(F32) + gelu_value(z)).astype(BF16)
                for lo, hi, step in GROUPS:
                    if j + 1 == hi:
                        for part in range(lo, hi, step):
                            f_copy(m, pl.ds(part, step)).start()
        share(0, m)
        for j in range(NT):
            cols = slice(j * TN, (j + 1) * TN)
            slopes[rows, cols] = gelu_slope(zs[rows, cols])

    def backward(m, send):
        rows = chunk_rows(m)
        total = jnp.zeros((R, TN), F32)
        for j in range(NT):
            cols = slice(j * TN, (j + 1) * TN)
            z = zs[rows, cols]
            delta = (ys[m, j].astype(F32) * slopes[rows, cols]).astype(BF16)
            ds[rows, cols] = delta
            lhs[1, :R, cols] = delta
            total = total + delta.astype(F32) * z
        if send:
            rinv = rinvs[rows, :1]
            pull = jnp.sum(total, axis=-1, keepdims=True) * (1.0 / D) * rinv
            padded = lhs[1]
            for j in range(NT):
                cols = slice(j * TN, (j + 1) * TN)
                dn = jnp.dot(padded, wt[:, cols], preferred_element_type=F32)[:R]
                xj = xs[m, j].astype(F32)
                dy = ys[m, j].astype(F32) + rinv * (dn * gain[:, cols] - xj * pull)
                sendb[m, j] = dy.astype(BF16)
                for lo, hi, step in GROUPS:
                    if j + 1 == hi:
                        for part in range(lo, hi, step):
                            b_copy(m, pl.ds(part, step)).start()
        share(1, m)

    def forward_step(m):
        @pl.when(s > 0)
        def _():
            f_copy(m, whole).wait_recv()

        @pl.when(first)
        def _():
            loaded(xs, m)

        @pl.when(first & (m == 0))
        def _():
            forward(m, True, True)

        @pl.when((s < SECTIONS - 1) & ((s > 0) | (m > 0)))
        def _():
            forward(m, True)

        @pl.when(last)
        def _():
            forward(m, False)

    def backward_step(m):
        @pl.when(s < SECTIONS - 1)
        def _():
            b_copy(m, whole).wait_recv()

        @pl.when(last & (m == 0))
        def _():
            cot_whole(0).wait_recv()

        @pl.when(last & (m == 1))
        def _():
            cot_whole(1).wait_recv()

        @pl.when(s > 0)
        def _():
            backward(m, True)

        @pl.when(first)
        def _():
            backward(m, False)

    def slab_of(f, k, tile, count):
        return gram.at[f, pl.ds(k + tile, count), pl.ds(pl.multiple_of(k * SLAB, SLAB), SLAB), :]

    def zp_copy(f, z):
        src = slab_of(f, 2 * z + yc, 0, KEPT)
        return remote(src, zp.at[f, zc], zp_send.at[f, z], zp_recv.at[f, zc], zpeer(z))

    def zp_arrival(f, z):
        return remote(zp.at[f, z], zp.at[f, z], zp_send.at[f, z], zp_recv.at[f, z], zpeer(z))

    def gp_copy(f, k, send_sem, device):
        part = ag.at[f, k, pl.ds(0, SPLIT), :]
        return remote(part, part, send_sem, gp_recv.at[f, k], device)

    def gq_copy(f, k, send_sem, device):
        part = ag.at[f, k, pl.ds(SPLIT, ZY * SLAB), :]
        return remote(part, part, send_sem, gq_recv.at[f, k], device)

    def gp_z(f, z):
        return gp_copy(f, chip, gp_zsend.at[f, z], zpeer(z))

    def gp_y(f, z):
        return gp_copy(f, 2 * z + yc, gp_ysend.at[f, z], ypeer)

    def gq_y(f):
        return gq_copy(f, chip, gq_ysend.at[f], ypeer)

    def gq_z(f, z):
        return gq_copy(f, chip, gq_zsend.at[f, z], zpeer(z))

    def gq_f(f, z):
        return gq_copy(f, 2 * zc + 1 - yc, gq_fsend.at[f, z], zpeer(z))

    def other_z(fn):
        def body(i, _):
            fn((zc + i) % 4)
            return 0

        lax.fori_loop(1, 4, body, 0)

    def gram_send(f):
        def landed(m, _):
            for p in range(3):
                sib_copy(f, m, p).wait_recv()
            return 0

        lax.fori_loop(0, M - 1, landed, 0)
        sib_copy(f, M - 1, 0).wait_recv()
        early = ROWS - R
        store = ns if f == 0 else ds
        own = store[:, pl.ds(pl.multiple_of(core * BLK, BLK), BLK)]
        dims = (((0,), (0,)), ((), ()))
        for i in range(1, 5):
            k = 2 * ((zc + i) % 4) + yc
            cut = pl.ds(pl.multiple_of(k * SLAB, SLAB), SLAB)
            own_cut = store[:, pl.ds(pl.multiple_of(core * BLK + k * SLAB, SLAB), SLAB)]
            part = lax.dot_general(own_cut, own, dims, preferred_element_type=F32)
            part = part + lax.dot_general(sib[f, 0, :, cut], sib[f, 0], dims, preferred_element_type=F32)
            for p in (1, 2):
                part = part + lax.dot_general(
                    sib[f, p, :early, cut], sib[f, p, :early, :], dims, preferred_element_type=F32
                )
            partial[i - 1] = part
        for p in (1, 2):
            sib_copy(f, M - 1, p).wait_recv()
        rest = jnp.concatenate([sib[f, 1, early:, :], sib[f, 2, early:, :]], axis=0)
        for i in range(1, 5):
            q = (zc + i) % 4
            k = 2 * q + yc
            cut = pl.ds(pl.multiple_of(k * SLAB, SLAB), SLAB)
            rest_cut = jnp.concatenate([sib[f, 1, early:, cut], sib[f, 2, early:, cut]], axis=0)
            part = partial[i - 1] + lax.dot_general(rest_cut, rest, dims, preferred_element_type=F32)
            part = part.astype(BF16)
            for t in range(CHIPS):
                tile = part[:, t * SLAB : (t + 1) * SLAB]
                gram[f, t, cut, :] = tile
                if t < KEPT - 1:
                    gram[f, t + CHIPS, cut, :] = tile
            if i < 4:
                zp_copy(f, q).start()

    def mine_tile(f, k, t):
        return gram[f, k + t, pl.ds(pl.multiple_of(k * SLAB, SLAB), SLAB), :].astype(F32)

    def sum_gather(f):
        other_z(lambda z: zp_arrival(f, z).wait_recv())
        ri = lax.broadcasted_iota(jnp.int32, (SLAB, SLAB), 0)
        ci = lax.broadcasted_iota(jnp.int32, (SLAB, SLAB), 1)
        eye = ri == ci

        def put(t, total):
            ag[f, chip, EXTRA + t * SLAB : EXTRA + (t + 1) * SLAB, :] = total.astype(BF16)

        for t in range(KEPT):
            total = mine_tile(f, chip, t)
            for i in range(1, 4):
                total = total + zp[f, (zc + i) % 4, t].astype(F32)
            total = total * (1.0 / ROW_TOTAL)
            if t == 0:
                diag = jnp.sum(jnp.where(eye, total, 0.0), axis=0, keepdims=True) + DAMPING
                high = diag.astype(BF16).astype(F32)
                row = lax.broadcasted_iota(jnp.int32, (EXTRA, SLAB), 0)
                extra = jnp.where(row == 0, high, jnp.where(row == 1, diag - high, 0.0))
                ag[f, chip, 0:EXTRA, :] = extra.astype(BF16)
                total = jnp.where(eye, 0.0, total)
            ag[f, chip, EXTRA + t * SLAB : EXTRA + (t + 1) * SLAB, :] = total.astype(BF16)
            if t == YZ - 1:
                other_z(lambda z: gp_z(f, z).start())
                gp_y(f, zc).start()
        gq_y(f).start()
        other_z(lambda z: gq_z(f, z).start())

    def assemble(f, k):
        here = pl.ds(pl.multiple_of(k * SLAB, SLAB), SLAB)
        for j in range(KEPT):
            there = pl.ds(pl.multiple_of(((k + j) % CHIPS) * SLAB, SLAB), SLAB)
            tile = ag[f, k, EXTRA + j * SLAB : EXTRA + (j + 1) * SLAB, :]
            full[here, there] = tile
            if 0 < j < KEPT - 1:
                full[there, here] = tile.T
        dv[:, here] = jnp.sum(ag[f, k, 0:EXTRA, :].astype(F32), axis=0, keepdims=True)

    def gathered(f, k):
        gp_copy(f, k, gp_ysend.at[f, 0], ypeer).wait_recv()
        gq_copy(f, k, gq_ysend.at[f], ypeer).wait_recv()

    def roots(f, out):
        across = 2 * zc + 1 - yc

        def pass_on(z):
            gp_copy(f, 2 * z + yc, gp_ysend.at[f, z], ypeer).wait_recv()
            gp_y(f, z).start()

        pass_on((zc + 1) % 4)
        gathered(f, across)
        other_z(lambda z: gq_f(f, z).start())
        pass_on((zc + 3) % 4)
        pass_on((zc + 2) % 4)
        assemble(f, chip)
        assemble(f, across)

        def direct(z):
            gq_copy(f, 2 * z + yc, gq_ysend.at[f], ypeer).wait_recv()
            assemble(f, 2 * z + yc)

        def indirect(z):
            gathered(f, 2 * z + 1 - yc)
            assemble(f, 2 * z + 1 - yc)

        other_z(direct)
        other_z(indirect)
        diag = dv[...]
        ones = jnp.ones((16, BLK), BF16)
        bound = jnp.abs(diag) + jnp.dot(ones, jnp.abs(full[...]), preferred_element_type=F32)[:1]
        scale = 1.0 / jnp.max(bound, axis=1, keepdims=True)
        mine = pl.ds(pl.multiple_of(chip * SLAB, SLAB), SLAB)
        ri = lax.broadcasted_iota(jnp.int32, (SLAB, BLK), 0)
        ci = lax.broadcasted_iota(jnp.int32, (SLAB, BLK), 1)
        eye = ci == ri + chip * SLAB
        scaled_diag = diag * scale
        off = full[mine, :].astype(F32) * scale
        slab[0] = off
        slab[1] = jnp.where(eye, scaled_diag, off)

        def times(u):
            u_diag = jnp.sum(jnp.where(eye, u, 0.0), axis=1, keepdims=True)
            u_off = jnp.where(eye, 0.0, u).astype(BF16)
            prod = jnp.dot(u_off, full[...], preferred_element_type=F32) * scale
            return prod + u_diag * slab[0] + u * scaled_diag

        u = times(0.0625 * slab[1]) - 0.5625 * slab[1]
        u = times(u) + 1.6875 * slab[1]
        u = times(u) - 2.4375 * slab[1]
        ztile[f] = u + jnp.where(eye, 2.25, 0.0)
        cols = pl.ds(pl.multiple_of(core * BLK, BLK), BLK)
        to_sibling(f, out).start()
        to_out(f, out).start()

    def to_sibling(f, out):
        cols = pl.ds(pl.multiple_of(core * BLK, BLK), BLK)
        return pltpu.make_async_remote_copy(
            src_ref=ztile.at[f, pl.ds(pl.multiple_of((1 - core) * HALF, HALF), HALF), :], dst_ref=out.at[:, cols],
            send_sem=out_send.at[f], recv_sem=out_recv.at[f], device_id=sibling, device_id_type=MESH,
        )

    def to_out(f, out):
        cols = pl.ds(pl.multiple_of(core * BLK, BLK), BLK)
        return pltpu.make_async_copy(
            ztile.at[f, pl.ds(pl.multiple_of(core * HALF, HALF), HALF), :], out.at[:, cols], own_sem.at[f]
        )

    @pl.when(s >= 4)
    def _():
        transpose_weight()

    lag = jnp.minimum(M, (SECTIONS - 1 - s) * LAG)

    def first_half(i, _):
        forward_step(i)

        @pl.when(i >= lag)
        def _():
            backward_step(i - lag)

        return 0

    lax.fori_loop(0, M, first_half, 0)

    @pl.when((s >= 1) & (s < 4))
    def _():
        transpose_weight()

    @pl.when(s <= 4)
    def _():
        gram_send(0)

    @pl.when(s <= 3)
    def _():
        sum_gather(0)

    @pl.when(s <= 2)
    def _():
        roots(0, act_out)

    def second_half(i, _):
        backward_step(i)

        @pl.when((s == 4) & (i == 2))
        def _():
            sum_gather(0)

        return 0

    lax.fori_loop(M - lag, M, second_half, 0)

    @pl.when(s >= 5)
    def _():
        gram_send(0)

    gram_send(1)

    @pl.when(s >= 5)
    def _():
        sum_gather(0)

    sum_gather(1)

    @pl.when(s >= 3)
    def _():
        roots(0, act_out)

    roots(1, grad_out)

    for f, out in ((0, act_out), (1, grad_out)):
        to_out(f, out).wait()
        to_sibling(f, out).wait()

    def sent(m, _):
        @pl.when(s < SECTIONS - 1)
        def _():
            f_copy(m, whole).wait_send()

        @pl.when(s > 0)
        def _():
            b_copy(m, whole).wait_send()

        for p in range(3):
            sib_copy(0, m, p).wait_send()
            sib_copy(1, m, p).wait_send()
        return 0

    lax.fori_loop(0, M, sent, 0)
    @pl.when(last)
    def _():
        cot_whole(0).wait_send()
        cot_whole(1).wait_send()

    for f in range(2):

        def z_sent(z):
            zp_copy(f, z).wait_send()
            gp_z(f, z).wait_send()
            gp_y(f, z).wait_send()
            gq_z(f, z).wait_send()
            gq_f(f, z).wait_send()

        other_z(z_sent)
        gp_y(f, zc).wait_send()
        gq_y(f).wait_send()


def copy_kernel(act, grad, act_out, grad_out, held, sems):
    loads = [pltpu.make_async_copy(act, held.at[0], sems.at[0]), pltpu.make_async_copy(grad, held.at[1], sems.at[1])]
    stores = [pltpu.make_async_copy(held.at[0], act_out, sems.at[2]), pltpu.make_async_copy(held.at[1], grad_out, sems.at[3])]
    for cp in loads:
        cp.start()
    for load, store in zip(loads, stores):
        load.wait()
        store.start()
    for cp in stores:
        cp.wait()


def shards(tokens, cotangent, gain, weight):
    out = jax.ShapeDtypeStruct((HALF, D), F32)
    dma = pltpu.SemaphoreType.DMA
    anywhere = pl.BlockSpec(memory_space=pl.ANY)
    chunks = (M, R, D)
    act, grad = pl.pallas_call(
        kernel,
        out_shape=(out, out),
        in_specs=[anywhere, anywhere, pl.BlockSpec(memory_space=pltpu.VMEM), anywhere],
        out_specs=(anywhere, anywhere),
        scratch_shapes=[
            pltpu.VMEM((D, D), BF16),
            pltpu.VMEM((D, D), BF16),
            pltpu.VMEM((M, NT, R, TN), BF16),
            pltpu.VMEM((M, NT, R, TN), BF16),
            pltpu.VMEM((M, NT, R, TN), BF16),
            pltpu.VMEM((M, NT, R, TN), BF16),
            pltpu.VMEM((ROWS, D), F32),
            pltpu.VMEM((ROWS, D), F32),
            pltpu.VMEM((ROWS, D), BF16),
            pltpu.VMEM((ROWS, D), BF16),
            pltpu.VMEM((ROWS, 128), F32),
            pltpu.VMEM((2, 3, ROWS, BLK), BF16),
            pltpu.VMEM((4, SLAB, BLK), F32),
            pltpu.VMEM((2, CHIPS + KEPT - 1, BLK, SLAB), BF16),
            pltpu.VMEM((2, 4, KEPT, SLAB, SLAB), BF16),
            pltpu.VMEM((2, CHIPS, EXTRA + KEPT * SLAB, SLAB), BF16),
            pltpu.VMEM((BLK, BLK), BF16),
            pltpu.VMEM((1, BLK), F32),
            pltpu.VMEM((2, SLAB, BLK), F32),
            pltpu.VMEM((2, SLAB, BLK), F32),
            pltpu.VMEM((2, PAD, D), BF16),
            dma((NT,)),
            dma((2,)),
            dma((M,)),
            dma((M,)),
            dma((M,)),
            dma((M,)),
            dma((2, 3, M)),
            dma((2, 3, M)),
            dma((2, 4)),
            dma((2, 4)),
            dma((2, 4)),
            dma((2, 4)),
            dma((2, CHIPS)),
            dma((2,)),
            dma((2, 4)),
            dma((2, 4)),
            dma((2, CHIPS)),
            dma((2,)),
            dma((2,)),
            dma((2,)),
            dma((2,)),
        ],
        name="refresh",
        compiler_params=pltpu.CompilerParams(
            collective_id=0, has_side_effects=True, vmem_limit_bytes=58 * 2**20
        ),
    )(tokens.reshape(chunks), cotangent.reshape(chunks), gain, weight)
    return pl.pallas_call(
        copy_kernel,
        out_shape=(out, out),
        in_specs=[anywhere] * 2,
        out_specs=(anywhere, anywhere),
        scratch_shapes=[pltpu.VMEM((2, HALF, D), F32), dma((4,))],
        name="results",
    )(act, grad)


def solution(mesh):
    return jax.shard_map(
        shards,
        mesh=mesh,
        in_specs=(P(None, "dp", None), P(None, "dp", None), P("section", None), P("section", None)),
        out_specs=(P(("section", "dp"), None), P(("section", "dp"), None)),
        check_vma=False,
    )
```
